256 devices in a mesh: section: 2 (over core), dp: 16 (over z, x_hi), mp: 8 (over y, x_lo).
Axes of the slice: x: 4 (x_hi: 2, x_lo: 2; x = x_hi * 2 + x_lo), y: 4, z: 8, core: 2. Of those that a mesh axis runs over, the one named last changes fastest.
Arguments:
- token_ids: int32 [4, 512], replicated, may hold values from 0 to 65535
- next_ids: int32 [4, 512], replicated, may hold values from 0 to 65535
- embed_table: bfloat16 [65536, 7168], P(('section', 'dp'), 'mp'), may hold values from -6 to 6
- norm_gain: float32 [2, 7168], P('section'), may hold values from 0.5 to 1.5
- w_gate: bfloat16 [2, 7168, 1024], P('section', None, 'mp'), may hold values from -0.0625 to 0.0625
- w_up: bfloat16 [2, 7168, 1024], P('section', None, 'mp'), may hold values from -0.0625 to 0.0625
- w_down: bfloat16 [2, 1024, 7168], P('section', 'mp'), may hold values from -0.1875 to 0.1875
- mtp_gain: float32 [2, 7168], replicated, may hold values from 0.5 to 1.5
- main_cot: bfloat16 [4, 512, 7168], P(None, 'dp', 'mp'), may hold values from -6 to 6
- mtp_cot: bfloat16 [4, 512, 7168], P(None, 'dp', 'mp'), may hold values from -6 to 6
Outputs:
- embed_grad: bfloat16 [65536, 7168], P(('section', 'dp'), 'mp')
The draws below stay inside these ranges and needn't reach their ends.
All inputs are finite; a program needn't handle non-finite values.
Results may differ from the reference program's by a relative error of at most 0.022.
Values may be sent and summed in bfloat16 or wider, within the bound.
A program may use at most 128 MiB of HBM per device.

```python
import math
import jax
import jax.numpy as jnp
import numpy as np
from jax import lax

D = 7168
FF = 1024
MB = 4
TOKENS = 512
VOCAB = 65536
N_SECTION = 2
N_MP = 8


def plant(values, stream_key, least, largest):
    longest = values.shape.index(max(values.shape))
    spots = []
    for shift in (0, 1):
        where = [jax.random.randint(jax.random.fold_in(stream_key, axis), (), 0, length) for axis, length in enumerate(values.shape)]
        where[longest] = (where[longest] + shift) % values.shape[longest]
        spots.append(tuple(where))
    return values.at[spots[0]].set(least).at[spots[1]].set(largest)


def block_scale(own_key, extent, pieces, low, high):
    factor_of = 1.0
    for position, shards_of in pieces:
        heights = jax.random.uniform(jax.random.fold_in(jax.random.fold_in(own_key, 6), position), (shards_of,), jnp.float32, low / len(pieces), high / len(pieces))
        factor_of = factor_of * jnp.repeat(jnp.exp(heights), extent[position] // shards_of).reshape((-1,) + (1,) * (len(extent) - 1 - position))
    return factor_of


def rank_table(count, skew):
    weights = [(1 << 20) // math.isqrt(grade ** skew) + 1 for grade in range(1, count + 1)]
    width = 1 + sum(weights) // (1 << 30)
    return np.cumsum(np.array([max(1, weight // width) for weight in weights]))


def ranked_ids(own_key, shape, count, lean):
    listing = rank_table(count, lean)
    pick = jax.random.randint(jax.random.fold_in(own_key, 1), shape, 0, int(listing[count - 1]))
    standing = jnp.searchsorted(jnp.asarray(listing, jnp.int32), pick, side="right")
    return jax.random.permutation(jax.random.fold_in(own_key, 2), count)[standing].astype(jnp.int32)


def normal_values(stream_key, shape, spread, most, pieces=(), kind=jnp.bfloat16):
    values = jax.random.normal(stream_key, shape, jnp.float32) * spread
    if len(pieces) > 0:
        values = block_scale(stream_key, shape, pieces, -0.22, 0.18) * values
    return jnp.clip(values, min=-most, max=most).astype(kind)


def setup_inputs(seed: int = 0) -> dict:
    key_of = jax.random.split(jax.random.key(seed), 11)
    token_ids = plant(ranked_ids(key_of[0], (MB, TOKENS), VOCAB, 2), jax.random.fold_in(key_of[0], 3), 0, VOCAB - 1).astype(jnp.int32)
    next_ids = plant(ranked_ids(key_of[1], (MB, TOKENS), VOCAB, 2), jax.random.fold_in(key_of[1], 3), 0, VOCAB - 1).astype(jnp.int32)
    embed_table = normal_values(key_of[2], (VOCAB, D), 1.0, 6.0, ((0, 32), (1, 8)))
    norm_gain = jnp.clip(1.0 + 0.1 * jax.random.normal(key_of[3], (N_SECTION, D), jnp.float32), 0.5, 1.5)
    w_gate = normal_values(key_of[4], (N_SECTION, D, FF), D ** -0.5, 0.0625, ((0, 2), (2, 8)))
    w_up = normal_values(key_of[5], (N_SECTION, D, FF), D ** -0.5, 0.0625, ((0, 2), (2, 8)))
    w_down = normal_values(key_of[6], (N_SECTION, FF, D), FF ** -0.5, 0.1875, ((0, 2), (1, 8)))
    mtp_gain = jnp.clip(1.0 + 0.1 * jax.random.normal(key_of[7], (2, D), jnp.float32), 0.5, 1.5)
    main_cot = normal_values(key_of[8], (MB, TOKENS, D), 1.0, 6.0, ((1, 16), (2, 8)))
    mtp_cot = normal_values(key_of[9], (MB, TOKENS, D), 1.0, 6.0, ((1, 16), (2, 8)))
    return dict(token_ids=token_ids, next_ids=next_ids, embed_table=embed_table, norm_gain=norm_gain, w_gate=w_gate, w_up=w_up, w_down=w_down, mtp_gain=mtp_gain, main_cot=main_cot, mtp_cot=mtp_cot)


EPS = 1e-06

def inverse_rms(values):
    return lax.rsqrt(lax.optimization_barrier(jnp.mean(values * values, axis=-1, keepdims=True)) + EPS)

def norm_back(values, weight):
    inverse = inverse_rms(values)
    return inverse * weight - values * (inverse * inverse * inverse) * lax.optimization_barrier(jnp.mean(values * weight, axis=-1, keepdims=True))

def rounded_sum(terms):
    rounded = lax.optimization_barrier(terms.astype(jnp.bfloat16))
    return lax.optimization_barrier(jnp.sum(rounded.astype(jnp.float32), axis=0))

def split_hidden(hidden):
    return hidden.astype(jnp.float32).reshape(hidden.shape[0], N_MP, hidden.shape[1] // N_MP)

def block_start(stream, gain, gate_weight, up_weight):
    stream_f = stream.astype(jnp.float32)
    normed = (stream_f * inverse_rms(stream_f) * gain).astype(jnp.bfloat16)
    gate_out = jnp.dot(normed, gate_weight, preferred_element_type=jnp.float32)
    up_out = jnp.dot(normed, up_weight, preferred_element_type=jnp.float32)
    return (stream_f, gate_out, up_out)

def forward_block(stream, gain, gate_weight, up_weight, down_weight):
    stream_f, gate_out, up_out = block_start(stream, gain, gate_weight, up_weight)
    hidden = (jax.nn.silu(gate_out) * up_out).astype(jnp.bfloat16)
    down_parts = down_weight.astype(jnp.float32).reshape(N_MP, hidden.shape[1] // N_MP, down_weight.shape[1])
    terms = jnp.einsum('tpf,pfd->ptd', split_hidden(hidden), down_parts)
    return (stream_f + rounded_sum(terms)).astype(jnp.bfloat16)

def backward_block(stream, grad_out, gain, gate_weight, up_weight, down_weight):
    stream_f, gate_out, up_out = block_start(stream, gain, gate_weight, up_weight)
    sigmoid_gate = jax.nn.sigmoid(gate_out)
    activated = gate_out * sigmoid_gate
    grad_hidden = jnp.dot(grad_out, down_weight.T, preferred_element_type=jnp.float32)
    grad_gate = (grad_hidden * up_out * sigmoid_gate * (1.0 + gate_out * (1.0 - sigmoid_gate))).astype(jnp.bfloat16)
    grad_up = (grad_hidden * activated).astype(jnp.bfloat16)
    model_width = gate_weight.shape[0]
    part_size = gate_weight.shape[1] // N_MP
    gate_parts = gate_weight.astype(jnp.float32).reshape(model_width, N_MP, part_size)
    up_parts = up_weight.astype(jnp.float32).reshape(model_width, N_MP, part_size)
    terms = jnp.einsum('tpf,dpf->ptd', split_hidden(grad_gate), gate_parts) + jnp.einsum('tpf,dpf->ptd', split_hidden(grad_up), up_parts)
    return grad_out.astype(jnp.float32) + norm_back(stream_f, gain * rounded_sum(terms))

def mixed_inputs(hidden_rows, embedded, mtp_gain):
    hidden_f = hidden_rows.astype(jnp.float32)
    embedded_f = embedded.astype(jnp.float32)
    return (hidden_f * inverse_rms(hidden_f) * mtp_gain[0] + embedded_f * inverse_rms(embedded_f) * mtp_gain[1]).astype(jnp.bfloat16)

def reference(token_ids, next_ids, embed_table, norm_gain, w_gate, w_up, w_down, mtp_gain, main_cot, mtp_cot):
    mtp_layer = N_SECTION - 1
    main_grads = []
    next_grads = []
    for number in range(MB):
        stream = embed_table[token_ids[number]]
        embedded = embed_table[next_ids[number]]
        saved_inputs = []
        for layer_index in range(mtp_layer):
            saved_inputs.append(stream)
            stream = forward_block(stream, norm_gain[layer_index], w_gate[layer_index], w_up[layer_index], w_down[layer_index])
        mixed = mixed_inputs(stream, embedded, mtp_gain)
        grad_mixed = backward_block(mixed, mtp_cot[number], norm_gain[mtp_layer], w_gate[mtp_layer], w_up[mtp_layer], w_down[mtp_layer])
        grad_stream = main_cot[number].astype(jnp.float32) + norm_back(stream.astype(jnp.float32), mtp_gain[0] * grad_mixed)
        next_grads.append(norm_back(embedded.astype(jnp.float32), mtp_gain[1] * grad_mixed).astype(jnp.bfloat16))
        grad_stream = grad_stream.astype(jnp.bfloat16)
        for layer_index in reversed(range(mtp_layer)):
            grad_stream = backward_block(saved_inputs[layer_index], grad_stream, norm_gain[layer_index], w_gate[layer_index], w_up[layer_index], w_down[layer_index]).astype(jnp.bfloat16)
        main_grads.append(grad_stream)
    all_ids = jnp.concatenate([token_ids.reshape(-1), next_ids.reshape(-1)]).astype(jnp.int32)
    all_rows = jnp.concatenate([jnp.stack(main_grads).reshape(-1, D), jnp.stack(next_grads).reshape(-1, D)]).astype(jnp.float32)
    column_blocks = all_rows.reshape(-1, N_MP, D // N_MP).transpose(1, 0, 2)

    def table_block(block_rows):
        return jax.ops.segment_sum(block_rows, all_ids, num_segments=VOCAB).astype(jnp.bfloat16)
    tables = lax.map(table_block, column_blocks)
    return tables.transpose(1, 0, 2).reshape(VOCAB, D)
```

```python
import functools

import jax
import jax.numpy as jnp
from jax import lax
from jax.experimental import pallas as pl
from jax.experimental.pallas import tpu as pltpu
from jax.sharding import PartitionSpec as P

EPS = 1e-06


def from_behind(value, axis, steps):
    count = lax.axis_size(axis)
    first, last = (max(0, -steps), min(count, count - steps))
    return lax.ppermute(value, axis, [(source, source + steps) for source in range(first, last)])


def inverse_rms(values):
    return lax.rsqrt(jnp.mean(values * values, axis=-1, keepdims=True) + EPS)


def norm_back(values, weight):
    inverse = inverse_rms(values)
    return inverse * weight - values * (inverse * inverse * inverse) * jnp.mean(
        values * weight, axis=-1, keepdims=True
    )


def mixed_inputs(hidden_rows, embedded, mtp_gain):
    hidden_f = hidden_rows.astype(jnp.float32)
    embedded_f = embedded.astype(jnp.float32)
    return (
        hidden_f * inverse_rms(hidden_f) * mtp_gain[0]
        + embedded_f * inverse_rms(embedded_f) * mtp_gain[1]
    ).astype(jnp.bfloat16)


def send_up(values):
    return from_behind(values, "section", -1)


def send_down(values):
    return from_behind(values, "section", 1)


def narrow(terms):
    return lax.psum(terms.astype(jnp.bfloat16), "mp").astype(jnp.float32)


def forward_block(stream, gain, gate_weight, up_weight, down_weight):
    whole = stream.astype(jnp.float32)
    normed = (whole * inverse_rms(whole) * gain).astype(jnp.bfloat16)
    gate_out = jnp.dot(normed, gate_weight, preferred_element_type=jnp.float32)
    up_out = jnp.dot(normed, up_weight, preferred_element_type=jnp.float32)
    hidden = (jax.nn.silu(gate_out) * up_out).astype(jnp.bfloat16)
    term = lax.optimization_barrier(
        jnp.dot(hidden, down_weight, preferred_element_type=jnp.float32).astype(jnp.bfloat16)
    )
    return (stream.astype(jnp.float32) + narrow(term.astype(jnp.float32))).astype(jnp.bfloat16)


def backward_block(stream, grad_out, gain, gate_weight, up_weight, down_weight):
    whole, grad_whole = (stream, grad_out)
    whole_f = whole.astype(jnp.float32)
    normed = (whole_f * inverse_rms(whole_f) * gain).astype(jnp.bfloat16)
    gate_out = jnp.dot(normed, gate_weight, preferred_element_type=jnp.float32)
    up_out = jnp.dot(normed, up_weight, preferred_element_type=jnp.float32)
    sigmoid_gate = jax.nn.sigmoid(gate_out)
    activated = gate_out * sigmoid_gate
    contract = (((1,), (1,)), ((), ()))
    grad_hidden = lax.dot_general(
        grad_whole, down_weight, contract, preferred_element_type=jnp.float32
    )
    grad_gate = (
        grad_hidden * up_out * sigmoid_gate * (1.0 + gate_out * (1.0 - sigmoid_gate))
    ).astype(jnp.bfloat16)
    grad_up = (grad_hidden * activated).astype(jnp.bfloat16)
    back = lax.dot_general(grad_gate, gate_weight, contract, preferred_element_type=jnp.float32)
    back = back + lax.dot_general(grad_up, up_weight, contract, preferred_element_type=jnp.float32)
    back = lax.optimization_barrier(back.astype(jnp.bfloat16)).astype(jnp.float32)
    grad_normed = narrow(back)
    return grad_out.astype(jnp.float32) + norm_back(stream.astype(jnp.float32), gain * grad_normed)


def dense_body(
    token_ids, next_ids, embed_table, norm_gain, w_gate, w_up, w_down, mtp_gain, main_cot, mtp_cot
):
    sections = lax.axis_size("section")
    replicas = lax.axis_size("dp")
    section_index = lax.axis_index("section")
    replica = lax.axis_index("dp")
    mp_index = lax.axis_index("mp")
    batches = token_ids.shape[0]
    row_count = token_ids.shape[1] // replicas
    model_width = norm_gain.shape[1]
    vocab_rows = embed_table.shape[0]
    piece_width = embed_table.shape[1]
    is_first = section_index == 0
    is_last = section_index == sections - 1
    gain = norm_gain[0]
    gate_weight = w_gate[0]
    up_weight = w_up[0]
    down_weight = w_down[0]
    main_ids = token_ids.reshape(batches, replicas, row_count).transpose(1, 0, 2)
    after_ids = next_ids.reshape(batches, replicas, row_count).transpose(1, 0, 2)
    layout_ids = jnp.full((sections, replicas, batches, row_count), -1, jnp.int32)
    layout_ids = layout_ids.at[0].set(main_ids).at[sections - 1].set(after_ids)
    block_ids = layout_ids.reshape(-1)
    local_ids = block_ids - (section_index * replicas + replica) * vocab_rows
    inside = (local_ids >= 0) & (local_ids < vocab_rows)
    safe_ids = jnp.clip(local_ids, 0, vocab_rows - 1)
    picked = jnp.where(
        inside[:, None], jnp.take(embed_table, safe_ids, axis=0), jnp.zeros((), jnp.bfloat16)
    )
    own_piece = lax.psum_scatter(
        picked.astype(jnp.float32).astype(jnp.bfloat16),
        ("section", "dp"),
        scatter_dimension=0,
        tiled=True,
    ).astype(jnp.float32)
    own_piece = own_piece.astype(jnp.bfloat16).reshape(batches, row_count, piece_width)
    block_rows, main_full, mtp_full = (
        lax.all_gather(own_piece, "mp", axis=2, tiled=True),
        lax.all_gather(main_cot, "mp", axis=2, tiled=True),
        lax.all_gather(mtp_cot, "mp", axis=2, tiled=True),
    )
    local_rows = block_rows.shape[1]
    empty_rows = jnp.zeros((local_rows, model_width), jnp.bfloat16)
    empty_stack = jnp.zeros((batches, local_rows, model_width), jnp.bfloat16)
    ticks = batches + sections - 1

    def forward_tick(step_index, state_now):
        received, saved = state_now
        micro = step_index - section_index
        slot_index = jnp.clip(micro, 0, batches - 1)
        raw_rows = jnp.where(is_first, block_rows[slot_index], received)
        mixed = mixed_inputs(raw_rows, block_rows[slot_index], mtp_gain)
        block_in = jnp.where(is_last, mixed, raw_rows)
        result = forward_block(block_in, gain, gate_weight, up_weight, down_weight)
        active = (micro >= 0) & (micro < batches)
        saved = jnp.where(
            active, lax.dynamic_update_index_in_dim(saved, raw_rows, slot_index, 0), saved
        )
        return (send_down(result), saved)

    received, saved = lax.fori_loop(0, ticks, forward_tick, (empty_rows, empty_stack))

    def backward_tick(step_index, state_now):
        received, grads = state_now
        micro = step_index - (sections - 1 - section_index)
        slot_index = jnp.clip(micro, 0, batches - 1)
        raw_rows = saved[slot_index]
        embedded = block_rows[slot_index]
        mixed = mixed_inputs(raw_rows, embedded, mtp_gain)
        block_in = jnp.where(is_last, mixed, raw_rows)
        grad_out = jnp.where(is_last, mtp_full[slot_index], received)
        grad_in = backward_block(block_in, grad_out, gain, gate_weight, up_weight, down_weight)
        grad_main = main_full[slot_index].astype(jnp.float32) + norm_back(
            raw_rows.astype(jnp.float32), mtp_gain[0] * grad_in
        )
        grad_next = norm_back(embedded.astype(jnp.float32), mtp_gain[1] * grad_in)
        outgoing = jnp.where(is_last, grad_main, grad_in).astype(jnp.bfloat16)
        keeping = jnp.where(is_last, grad_next, grad_in).astype(jnp.bfloat16)
        active = (micro >= 0) & (micro < batches)
        grads = jnp.where(
            active, lax.dynamic_update_index_in_dim(grads, keeping, slot_index, 0), grads
        )
        return (send_up(outgoing), grads)

    received, grads = lax.fori_loop(0, ticks, backward_tick, (empty_rows, empty_stack))
    home = jnp.where(is_first | is_last, grads, jnp.zeros((), jnp.bfloat16))
    own_cols = lax.dynamic_slice_in_dim(home, mp_index * piece_width, piece_width, 2)
    everyone = lax.all_gather(
        own_cols.reshape(-1, piece_width), ("section", "dp"), axis=0, tiled=True
    )
    masked = jnp.where(inside[:, None], everyone.astype(jnp.float32), 0.0)
    table = jax.ops.segment_sum(masked, safe_ids, num_segments=vocab_rows)
    return table.astype(jnp.bfloat16)


MESH = pl.DeviceIdType.MESH
SLOTS = 16
BF = jnp.bfloat16
F32 = jnp.float32
COLS = (((1,), (1,)), ((), ()))
ROWS = (((0,), (0,)), ((), ()))


def dot(a, b):
    return jnp.dot(a, b, preferred_element_type=F32)


def dot_t(a, b):
    return lax.dot_general(a, b, COLS, preferred_element_type=F32)


def iota(shape, axis):
    return lax.broadcasted_iota(jnp.int32, shape, axis)


def greet(devices):
    barrier = pltpu.get_barrier_semaphore()
    for_all, count = devices

    def signal(step, carry):
        pl.semaphore_signal(barrier, inc=1, device_id=for_all(step), device_id_type=MESH)
        return carry

    lax.fori_loop(0, count, signal, 0)
    pl.semaphore_wait(barrier, count)


def remote(source, target, send_sem, recv_sem, device):
    return pltpu.make_async_remote_copy(
        src_ref=source,
        dst_ref=target,
        send_sem=send_sem,
        recv_sem=recv_sem,
        device_id=device,
        device_id_type=MESH,
    )


def to_column(row):
    count = row.shape[1]
    eye = iota((count, count), 0) == iota((count, count), 1)
    whole = jnp.broadcast_to(row, (count, count))
    return jnp.sum(jnp.where(eye, whole, jnp.zeros_like(whole)), axis=1, keepdims=True)


def to_row(column):
    count = column.shape[0]
    eye = iota((count, count), 0) == iota((count, count), 1)
    whole = jnp.broadcast_to(column, (count, count))
    return jnp.sum(jnp.where(eye, whole, jnp.zeros_like(whole)), axis=0, keepdims=True)


def gather_kernel(
    sections,
    replicas,
    parts,
    ids_ref,
    table_hbm,
    gate_hbm,
    up_hbm,
    down_hbm,
    rows_ref,
    slot_ref,
    lid_ref,
    over_ref,
    gu_out,
    down_out,
    table,
    first,
    rank,
    lid,
    onehot,
    send,
    recv,
    table_sem,
    local_sem,
    send_sem,
    recv_sem,
    weight_local,
    weight_send,
    weight_recv,
):
    section = lax.axis_index("section")
    replica = lax.axis_index("dp")
    part = lax.axis_index("mp")
    count = sections * replicas
    me = section * replicas + replica
    vocab_rows, width = table_hbm.shape
    hidden = gate_hbm.shape[1]
    tokens = ids_ref.shape[1]
    load = pltpu.make_async_copy(table_hbm, table, table_sem)
    load.start()

    def column_peer(step):
        other = lax.rem(me + 1 + step, count)
        return other, (other // replicas, lax.rem(other, replicas), part)

    def row_peer(step):
        other = lax.rem(part + 1 + step, parts)
        return other, (section, replica, other)

    def any_peer(step):
        column = column_peer(step)[1]
        row = row_peer(step - (count - 1))[1]
        is_column = step < count - 1
        return tuple(jnp.where(is_column, a, b) for a, b in zip(column, row))

    greet((any_peer, count - 1 + parts - 1))

    def weight_pieces(source, slot):
        features = pl.ds(pl.multiple_of(source * width, width), width)
        return (
            (gate_hbm.at[features, :], gu_out.at[slot, :, pl.ds(0, hidden)]),
            (up_hbm.at[features, :], gu_out.at[slot, :, pl.ds(hidden, hidden)]),
            (down_hbm.at[:, features], down_out.at[slot]),
        )

    def weight_copies(step):
        other, device = row_peer(step)
        return [
            remote(a, b, weight_send.at[i, step], weight_recv.at[i, part], device)
            for i, (a, b) in enumerate(weight_pieces(other, part))
        ]

    def weight_start(step, carry):
        for copy in weight_copies(step):
            copy.start()
        return carry

    lax.fori_loop(0, parts - 1, weight_start, 0)
    own_weights = [
        pltpu.make_async_copy(a, b, weight_local.at[i])
        for i, (a, b) in enumerate(weight_pieces(part, part))
    ]
    for copy in own_weights:
        copy.start()

    earlier = iota((tokens, tokens), 0) < iota((tokens, tokens), 1)

    def find_first(index, carry):
        row = ids_ref[pl.ds(index, 1), :]
        same = (to_column(row) == row) & earlier
        seen = jnp.max(jnp.where(same, 1.0, 0.0), axis=0, keepdims=True)
        first[pl.ds(index, 1), :] = 1.0 - seen
        return carry

    lax.fori_loop(0, count, find_first, 0)
    ids = ids_ref[...]
    shard = ids // vocab_rows
    is_first = first[...]

    def fill(index, most):
        held = jnp.where(shard == index, is_first, 0.0)
        return jnp.maximum(most, jnp.sum(held, axis=1, keepdims=True))

    most = lax.fori_loop(0, count, fill, jnp.zeros((count, 1), F32))
    over_ref[...] = jnp.broadcast_to(jnp.max(most, axis=0, keepdims=True), over_ref.shape)

    mine = jnp.where(shard == me, is_first, 0.0)
    triangle = jnp.where(earlier, 1.0, 0.0).astype(BF)
    rank[...] = jnp.where(mine > 0.0, dot(mine.astype(BF), triangle), -1.0)

    def find_lid(index, carry):
        row = ids_ref[pl.ds(index, 1), :] - me * vocab_rows + 1
        picks = rank[pl.ds(index, 1), :].astype(jnp.int32) == iota((SLOTS, tokens), 0)
        found = jnp.sum(
            jnp.where(picks, jnp.broadcast_to(row, picks.shape), 0), axis=1, keepdims=True
        )
        lid[pl.ds(pl.multiple_of(index * SLOTS, SLOTS), SLOTS), :] = jnp.broadcast_to(
            found - 1, (SLOTS, tokens)
        )
        return carry

    lax.fori_loop(0, count, find_lid, 0)
    for block in range(count * SLOTS // tokens):
        rows = pl.ds(block * tokens, tokens)
        eye = iota((tokens, tokens), 0) == iota((tokens, tokens), 1)
        row = jnp.sum(jnp.where(eye, lid[rows, :], 0), axis=0, keepdims=True)
        lid_ref[:, rows] = jnp.broadcast_to(row, (8, tokens))

    own_row = ids_ref[pl.ds(me, 1), :]
    own_first = first[pl.ds(me, 1), :]
    own_column = to_column(own_row)
    shard_row = own_row // vocab_rows
    first_column = to_column(own_first)
    counted = (own_column // vocab_rows == shard_row) & earlier & (first_column > 0.0)
    own_rank = jnp.sum(jnp.where(counted, 1, 0), axis=0, keepdims=True)
    slot_row = shard_row * SLOTS + own_rank
    leads = (own_column == own_row) & (own_first > 0.0)
    slot_column = jnp.sum(
        jnp.where(leads, jnp.broadcast_to(slot_row, leads.shape), 0), axis=1, keepdims=True
    )
    slot_ref[...] = jnp.broadcast_to(to_row(slot_column), (8, tokens))

    load.wait()
    group = tokens // SLOTS

    def column_copy(step):
        other, device = column_peer(step)
        return remote(
            send.at[other], recv.at[me], send_sem.at[step], recv_sem.at[me], device
        )

    def pick(block, carry):
        for inner in range(group):
            other = column_peer(block * group + inner)[0]
            wanted = lid[pl.ds(pl.multiple_of(other * SLOTS, SLOTS), SLOTS), :]
            for lane in range(vocab_rows // tokens):
                hit = wanted == iota(wanted.shape, 1) + lane * tokens
                onehot[pl.ds(inner * SLOTS, SLOTS), pl.ds(lane * tokens, tokens)] = jnp.where(
                    hit, 1.0, 0.0
                ).astype(BF)
        found = dot(onehot[...], table[...]).astype(BF)
        for inner in range(group):
            step = block * group + inner
            send[column_peer(step)[0]] = found[inner * SLOTS : (inner + 1) * SLOTS]

            @pl.when(step < count - 1)
            def _():
                column_copy(step).start()

        return carry

    lax.fori_loop(0, count // group, pick, 0)
    keep = pltpu.make_async_copy(send.at[me], recv.at[me], local_sem)
    keep.start()
    keep.wait()

    def arrive(step, carry):
        other, device = column_peer(step)
        remote(send.at[me], recv.at[other], send_sem.at[step], recv_sem.at[other], device).wait_recv()
        return carry

    lax.fori_loop(0, count - 1, arrive, 0)
    spread = jnp.where(slot_column == iota((tokens, count * SLOTS), 1), 1.0, 0.0).astype(BF)
    rows_ref[...] = dot(spread, recv[...].reshape(count * SLOTS, width)).astype(BF)

    def leave(step, carry):
        column_copy(step).wait_send()
        return carry

    lax.fori_loop(0, count - 1, leave, 0)

    def weight_wait(step, carry):
        other, device = row_peer(step)
        for i, (a, b) in enumerate(weight_pieces(other, other)):
            remote(a, b, weight_send.at[i, step], weight_recv.at[i, other], device).wait_recv()
        for copy in weight_copies(step):
            copy.wait_send()
        return carry

    lax.fori_loop(0, parts - 1, weight_wait, 0)
    for copy in own_weights:
        copy.wait()


def block_kernel(
    parts,
    rows_ref,
    main_cot_ref,
    mtp_cot_ref,
    gu_ref,
    down_ref,
    gain_ref,
    mtp_gain_ref,
    grad_ref,
    part_out,
    part_in,
    wide_in,
    early_out,
    early_in,
    narrow_in,
    wide_own,
    narrow_own,
    stat_out,
    stat_in,
    cross,
    hold,
    part_send,
    part_recv,
    early_send,
    early_recv,
    wide_send,
    wide_recv,
    narrow_send,
    narrow_recv,
    stat_send,
    stat_recv,
    cross_send,
    cross_recv,
):
    section = lax.axis_index("section")
    replica = lax.axis_index("dp")
    part = lax.axis_index("mp")
    tokens, width = rows_ref.shape
    hidden = down_ref.shape[1]
    model_width = parts * width
    features = pl.ds(pl.multiple_of(part * width, width), width)

    def peer(step):
        other = lax.rem(part + 1 + step, parts)
        return other, (section, replica, other)

    def any_peer(step):
        other = lax.rem(part + 1 + lax.rem(step, parts), parts)
        there = jnp.where(step < parts - 1, section, 1 - section)
        return (there, replica, other)

    greet((any_peer, 2 * parts - 1))

    gain = gain_ref[0:1, features]
    gain_main = mtp_gain_ref[0:1, features]
    gain_next = mtp_gain_ref[1:2, features]

    def total(values):
        return jnp.sum(values, axis=1, keepdims=True)

    def inverse(sum_of_squares):
        return lax.rsqrt(sum_of_squares / model_width + EPS)

    def scatter_start(outs, ins, send_sem, recv_sem):
        def one(step, carry):
            other, device = peer(step)
            remote(
                outs.at[other], ins.at[part], send_sem.at[step], recv_sem.at[part], device
            ).start()
            return carry

        lax.fori_loop(0, parts - 1, one, 0)

    def spread_start(own, ins, send_sem, recv_sem):
        def one(step, carry):
            device = peer(step)[1]
            remote(own, ins.at[part], send_sem.at[step], recv_sem.at[part], device).start()
            return carry

        lax.fori_loop(0, parts - 1, one, 0)

    def arrive(own, ins, send_sem, recv_sem):
        def one(step, carry):
            other, device = peer(step)
            copy = remote(own, ins.at[other], send_sem.at[step], recv_sem.at[other], device)
            copy.wait_recv()
            copy.wait_send()
            return carry

        lax.fori_loop(0, parts - 1, one, 0)

    def fill_parts(outs, ins, values_of):
        def one(step, carry):
            other = lax.rem(part + 1 + step, parts)
            outs[other] = values_of(other).astype(outs.dtype)
            return carry

        lax.fori_loop(0, parts, one, 0)
        ins[part] = outs[part]

    def summed(ins):
        value = ins[0].astype(F32)
        for index in range(1, parts):
            value = value + ins[index].astype(F32)
        return value

    def put_stats(columns):
        rows = [to_row(column) for column in columns]
        rows = rows + [jnp.zeros_like(rows[0])] * (8 - len(rows))
        stat_out[...] = jnp.concatenate(rows, axis=0)

    def get_stats(slot, count):
        value = stat_in[slot, 0]
        for index in range(1, parts):
            value = value + stat_in[slot, index]
        return [to_column(value[index : index + 1, :]) for index in range(count)]

    def share_stats(slot):
        stat_in[slot, part] = stat_out[...]
        spread_start(stat_out, stat_in.at[slot], stat_send, stat_recv.at[slot])

    def gate_up(normed):
        fill_parts(part_out, part_in, lambda index: dot(normed, gu_ref[index]))
        scatter_start(part_out, part_in, part_send, part_recv)

    def grad_hidden_start(grad):
        fill_parts(early_out, early_in, lambda index: dot_t(grad, down_ref[index]))
        scatter_start(early_out, early_in, early_send, early_recv)

    def grad_hidden_wait():
        arrive(early_out.at[0], early_in, early_send, early_recv)
        return summed(early_in)

    def backward(gate, up, grad_hidden):
        sigmoid = jax.nn.sigmoid(gate)
        grad_gate = grad_hidden * up * sigmoid * (1.0 + gate * (1.0 - sigmoid))
        grad_up = grad_hidden * gate * sigmoid
        wide_own[...] = jnp.concatenate([grad_gate, grad_up], axis=1).astype(BF)
        wide_in[part] = wide_own[...]
        spread_start(wide_own, wide_in, wide_send, wide_recv)
        arrive(wide_own, wide_in, wide_send, wide_recv)
        back = dot_t(wide_in[0], gu_ref[0])
        for index in range(1, parts):
            back = back + dot_t(wide_in[index], gu_ref[index])
        return back * gain

    @pl.when(section == 0)
    def _():
        rows = rows_ref[...].astype(F32)
        put_stats([total(rows * rows)])
        share_stats(0)
        gate_up((rows * gain).astype(BF))
        arrive(stat_out, stat_in.at[0], stat_send, stat_recv.at[0])
        scale = inverse(get_stats(0, 1)[0])
        arrive(part_out.at[0], part_in, part_send, part_recv)
        whole = summed(part_in) * scale
        hold[...] = whole
        gate = whole[:, :hidden]
        up = whole[:, hidden:]
        narrow_own[...] = (gate * jax.nn.sigmoid(gate) * up).astype(BF)
        narrow_in[part] = narrow_own[...]
        spread_start(narrow_own, narrow_in, narrow_send, narrow_recv)
        arrive(narrow_own, narrow_in, narrow_send, narrow_recv)
        out = rows_ref[...].astype(F32)
        for index in range(parts):
            out = out + dot(narrow_in[index], down_ref[index])
        cross[0] = out.astype(BF)
        over = remote(
            cross.at[0], cross.at[1], cross_send, cross_recv, (1 - section, replica, part)
        )
        over.start()
        main = cross[0].astype(F32)
        put_stats([total(main * main)])

        def tell(step, carry):
            other = lax.rem(part + step, parts)
            remote(
                stat_out,
                stat_in.at[1, part],
                stat_send.at[step],
                stat_recv.at[1, part],
                (1 - section, replica, other),
            ).start()
            return carry

        lax.fori_loop(0, parts, tell, 0)

        def told(step, carry):
            other = lax.rem(part + step, parts)
            remote(
                stat_out,
                stat_in.at[1, part],
                stat_send.at[step],
                stat_recv.at[1, part],
                (1 - section, replica, other),
            ).wait_send()
            return carry

        lax.fori_loop(0, parts, told, 0)
        over.wait_send()
        over.wait_recv()
        grad = cross[1]
        grad_hidden_start(grad)
        grad_hidden = grad_hidden_wait()
        whole = hold[...]
        scaled = backward(whole[:, :hidden], whole[:, hidden:], grad_hidden)
        rows = rows_ref[...].astype(F32)
        put_stats([total(rows * scaled)])
        share_stats(2)
        arrive(stat_out, stat_in.at[2], stat_send, stat_recv.at[2])
        mean = get_stats(2, 1)[0] / model_width
        scale = inverse(get_stats(0, 1)[0])
        result = grad.astype(F32) + scale * scaled - rows * (scale * scale * scale * mean)
        grad_ref[...] = result.astype(BF)

    @pl.when(section == 1)
    def _():
        rows = rows_ref[...].astype(F32)
        put_stats([total(rows * rows)])
        share_stats(0)
        grad_hidden_start(mtp_cot_ref[...])
        arrive(stat_out, stat_in.at[0], stat_send, stat_recv.at[0])
        scale_next = inverse(get_stats(0, 1)[0])
        grad_hidden = grad_hidden_wait()

        def heard(index, carry):
            remote(
                stat_out,
                stat_in.at[1, index],
                stat_send.at[0],
                stat_recv.at[1, index],
                (1 - section, replica, part),
            ).wait_recv()
            return carry

        lax.fori_loop(0, parts, heard, 0)
        over = remote(
            cross.at[0], cross.at[1], cross_send, cross_recv, (1 - section, replica, part)
        )
        over.wait_recv()
        scale_main = inverse(get_stats(1, 1)[0])
        main = cross[1].astype(F32)
        mixed = (main * scale_main * gain_main + rows * scale_next * gain_next).astype(BF)
        mixed = mixed.astype(F32)
        put_stats([total(mixed * mixed)])
        share_stats(2)
        gate_up((mixed * gain).astype(BF))
        arrive(stat_out, stat_in.at[2], stat_send, stat_recv.at[2])
        scale = inverse(get_stats(2, 1)[0])
        arrive(part_out.at[0], part_in, part_send, part_recv)
        whole = summed(part_in) * scale
        scaled = backward(whole[:, :hidden], whole[:, hidden:], grad_hidden)
        cot = mtp_cot_ref[...].astype(F32)
        next_weighted = rows * gain_next
        main_weighted = main * gain_main
        put_stats(
            [
                total(mixed * scaled),
                total(next_weighted * scaled),
                total(next_weighted * mixed),
                total(next_weighted * cot),
                total(main_weighted * scaled),
                total(main_weighted * mixed),
                total(main_weighted * cot),
            ]
        )
        share_stats(3)
        arrive(stat_out, stat_in.at[3], stat_send, stat_recv.at[3])
        s1, s2, s3, s4, s5, s6, s7 = get_stats(3, 7)
        slope = scale * scale * scale * (s1 / model_width)
        grad_mixed = cot + scale * scaled - mixed * slope
        mean_next = (s4 + scale * s2 - slope * s3) / model_width
        mean_main = (s7 + scale * s5 - slope * s6) / model_width
        grad_main = (
            main_cot_ref[...].astype(F32)
            + scale_main * (gain_main * grad_mixed)
            - main * (scale_main * scale_main * scale_main * mean_main)
        )
        cross[0] = grad_main.astype(BF)
        over.start()
        grad_next = scale_next * (gain_next * grad_mixed) - rows * (
            scale_next * scale_next * scale_next * mean_next
        )
        grad_ref[...] = grad_next.astype(BF)
        over.wait_send()


def scatter_kernel(
    sections, replicas, grad_ref, slot_ref, out_ref, send, send_sem, recv_sem, local_sem
):
    section = lax.axis_index("section")
    replica = lax.axis_index("dp")
    part = lax.axis_index("mp")
    count = sections * replicas
    me = section * replicas + replica
    tokens, width = grad_ref.shape

    def peer(step):
        other = lax.rem(me + 1 + step, count)
        return other, (other // replicas, lax.rem(other, replicas), part)

    greet((lambda step: peer(step)[1], count - 1))
    slots = count * SLOTS
    spread = jnp.where(slot_ref[0:1, :] == iota((slots, tokens), 0), 1.0, 0.0).astype(BF)
    send[...] = dot(spread, grad_ref[...]).astype(BF).reshape(count, SLOTS, width)

    def copy(step):
        other, device = peer(step)
        return remote(
            send.at[other], out_ref.at[me], send_sem.at[step], recv_sem.at[me], device
        )

    def start(step, carry):
        copy(step).start()
        return carry

    lax.fori_loop(0, count - 1, start, 0)
    keep = pltpu.make_async_copy(send.at[me], out_ref.at[me], local_sem)
    keep.start()
    keep.wait()

    def arrive(step, carry):
        other, device = peer(step)
        remote(
            send.at[me], out_ref.at[other], send_sem.at[step], recv_sem.at[other], device
        ).wait_recv()
        copy(step).wait_send()
        return carry

    lax.fori_loop(0, count - 1, arrive, 0)


def place_kernel(lid_ref, sums_ref, out_ref):
    rows = out_ref.shape[0]
    slots = sums_ref.shape[0]
    base = pl.program_id(0) * rows
    hit = lid_ref[0:1, :] == iota((rows, slots), 0) + base
    out_ref[...] = dot(jnp.where(hit, 1.0, 0.0).astype(BF), sums_ref[...]).astype(BF)


def vmem():
    return pl.BlockSpec(memory_space=pltpu.VMEM)


def anywhere():
    return pl.BlockSpec(memory_space=pl.ANY)


def dma(*shape):
    return pltpu.SemaphoreType.DMA(shape)


def params(collective_id):
    return pltpu.CompilerParams(
        collective_id=collective_id, has_side_effects=True, vmem_limit_bytes=56 << 20
    )


def fast_body(
    token_ids, next_ids, embed_table, norm_gain, w_gate, w_up, w_down, mtp_gain, main_cot, mtp_cot
):
    sections = lax.axis_size("section")
    replicas = lax.axis_size("dp")
    parts = lax.axis_size("mp")
    count = sections * replicas
    batches = token_ids.shape[0]
    row_count = token_ids.shape[1] // replicas
    tokens = batches * row_count
    vocab_rows, width = embed_table.shape
    hidden = w_gate.shape[2]
    ids = jnp.stack([token_ids, next_ids]).reshape(sections, batches, replicas, row_count)
    ids = ids.transpose(0, 2, 1, 3).reshape(count, tokens)
    slots = count * SLOTS
    rows, slot_row, lid_row, most, gate_up, down = pl.pallas_call(
        functools.partial(gather_kernel, sections, replicas, parts),
        out_shape=(
            jax.ShapeDtypeStruct((tokens, width), BF),
            jax.ShapeDtypeStruct((8, tokens), jnp.int32),
            jax.ShapeDtypeStruct((8, slots), jnp.int32),
            jax.ShapeDtypeStruct((8, 128), F32),
            jax.ShapeDtypeStruct((parts, width, 2 * hidden), BF),
            jax.ShapeDtypeStruct((parts, hidden, width), BF),
        ),
        in_specs=[vmem()] + [anywhere()] * 4,
        out_specs=(vmem(), vmem(), vmem(), vmem(), anywhere(), anywhere()),
        scratch_shapes=[
            pltpu.VMEM((vocab_rows, width), BF),
            pltpu.VMEM((count, tokens), F32),
            pltpu.VMEM((count, tokens), F32),
            pltpu.VMEM((slots, tokens), jnp.int32),
            pltpu.VMEM((tokens, vocab_rows), BF),
            pltpu.VMEM((count, SLOTS, width), BF),
            pltpu.VMEM((count, SLOTS, width), BF),
            pltpu.SemaphoreType.DMA,
            pltpu.SemaphoreType.DMA,
            dma(count),
            dma(count),
            dma(3),
            dma(3, parts),
            dma(3, parts),
        ],
        compiler_params=params(0),
        name="gather_rows",
    )(ids, embed_table, w_gate[0], w_up[0], w_down[0])
    grads = pl.pallas_call(
        functools.partial(block_kernel, parts),
        out_shape=jax.ShapeDtypeStruct((tokens, width), BF),
        in_specs=[vmem()] * 7,
        out_specs=vmem(),
        scratch_shapes=[
            pltpu.VMEM((parts, tokens, 2 * hidden), BF),
            pltpu.VMEM((parts, tokens, 2 * hidden), BF),
            pltpu.VMEM((parts, tokens, 2 * hidden), BF),
            pltpu.VMEM((parts, tokens, hidden), BF),
            pltpu.VMEM((parts, tokens, hidden), BF),
            pltpu.VMEM((parts, tokens, hidden), BF),
            pltpu.VMEM((tokens, 2 * hidden), BF),
            pltpu.VMEM((tokens, hidden), BF),
            pltpu.VMEM((8, tokens), F32),
            pltpu.VMEM((4, parts, 8, tokens), F32),
            pltpu.VMEM((2, tokens, width), BF),
            pltpu.VMEM((tokens, 2 * hidden), F32),
            dma(parts),
            dma(parts),
            dma(parts),
            dma(parts),
            dma(parts),
            dma(parts),
            dma(parts),
            dma(parts),
            dma(parts),
            dma(4, parts),
            pltpu.SemaphoreType.DMA,
            pltpu.SemaphoreType.DMA,
        ],
        compiler_params=params(1),
        name="blocks",
    )(
        rows,
        main_cot.reshape(tokens, width),
        mtp_cot.reshape(tokens, width),
        gate_up,
        down,
        norm_gain,
        mtp_gain,
    )
    sums = pl.pallas_call(
        functools.partial(scatter_kernel, sections, replicas),
        out_shape=jax.ShapeDtypeStruct((count, SLOTS, width), BF),
        in_specs=[vmem()] * 2,
        out_specs=vmem(),
        scratch_shapes=[
            pltpu.VMEM((count, SLOTS, width), BF),
            dma(count),
            dma(count),
            pltpu.SemaphoreType.DMA,
        ],
        compiler_params=params(2),
        name="scatter_rows",
    )(grads, slot_row)
    return most[0, 0], lid_row, sums.reshape(slots, width)


def place(lid_row, sums, vocab_rows):
    slots, width = sums.shape
    block = vocab_rows // 8
    return pl.pallas_call(
        place_kernel,
        grid=(vocab_rows // block,),
        out_shape=jax.ShapeDtypeStruct((vocab_rows, width), BF),
        in_specs=[
            pl.BlockSpec((8, slots), lambda i: (0, 0)),
            pl.BlockSpec((slots, width), lambda i: (0, 0)),
        ],
        out_specs=pl.BlockSpec((block, width), lambda i: (i, 0)),
        name="place_rows",
    )(lid_row, sums)


def body(*arguments):
    most, lid_row, sums = fast_body(*arguments)
    vocab_rows = arguments[2].shape[0]
    return lax.cond(
        most <= SLOTS,
        lambda *given: place(given[0], given[1], vocab_rows),
        lambda *given: dense_body(*given[2:]),
        lid_row,
        sums,
        *arguments,
    )


def solution(mesh):
    return jax.shard_map(
        body,
        mesh=mesh,
        in_specs=(
            P(),
            P(),
            P(("section", "dp"), "mp"),
            P("section", None),
            P("section", None, "mp"),
            P("section", None, "mp"),
            P("section", "mp", None),
            P(),
            P(None, "dp", "mp"),
            P(None, "dp", "mp"),
        ),
        out_specs=P(("section", "dp"), "mp"),
        check_vma=False,
    )
```

```python
import functools

import jax
import jax.numpy as jnp
from jax import lax
from jax.experimental import pallas as pl
from jax.experimental.pallas import tpu as pltpu
from jax.sharding import PartitionSpec as P

EPS = 1e-06


def from_behind(value, axis, steps):
    count = lax.axis_size(axis)
    first, last = (max(0, -steps), min(count, count - steps))
    return lax.ppermute(value, axis, [(source, source + steps) for source in range(first, last)])


def inverse_rms(values):
    return lax.rsqrt(jnp.mean(values * values, axis=-1, keepdims=True) + EPS)


def norm_back(values, weight):
    inverse = inverse_rms(values)
    return inverse * weight - values * (inverse * inverse * inverse) * jnp.mean(
        values * weight, axis=-1, keepdims=True
    )


def mixed_inputs(hidden_rows, embedded, mtp_gain):
    hidden_f = hidden_rows.astype(jnp.float32)
    embedded_f = embedded.astype(jnp.float32)
    return (
        hidden_f * inverse_rms(hidden_f) * mtp_gain[0]
        + embedded_f * inverse_rms(embedded_f) * mtp_gain[1]
    ).astype(jnp.bfloat16)


def send_up(values):
    return from_behind(values, "section", -1)


def send_down(values):
    return from_behind(values, "section", 1)


def narrow(terms):
    return lax.psum(terms.astype(jnp.bfloat16), "mp").astype(jnp.float32)


def forward_block(stream, gain, gate_weight, up_weight, down_weight):
    whole = stream.astype(jnp.float32)
    normed = (whole * inverse_rms(whole) * gain).astype(jnp.bfloat16)
    gate_out = jnp.dot(normed, gate_weight, preferred_element_type=jnp.float32)
    up_out = jnp.dot(normed, up_weight, preferred_element_type=jnp.float32)
    hidden = (jax.nn.silu(gate_out) * up_out).astype(jnp.bfloat16)
    term = lax.optimization_barrier(
        jnp.dot(hidden, down_weight, preferred_element_type=jnp.float32).astype(jnp.bfloat16)
    )
    return (stream.astype(jnp.float32) + narrow(term.astype(jnp.float32))).astype(jnp.bfloat16)


def backward_block(stream, grad_out, gain, gate_weight, up_weight, down_weight):
    whole, grad_whole = (stream, grad_out)
    whole_f = whole.astype(jnp.float32)
    normed = (whole_f * inverse_rms(whole_f) * gain).astype(jnp.bfloat16)
    gate_out = jnp.dot(normed, gate_weight, preferred_element_type=jnp.float32)
    up_out = jnp.dot(normed, up_weight, preferred_element_type=jnp.float32)
    sigmoid_gate = jax.nn.sigmoid(gate_out)
    activated = gate_out * sigmoid_gate
    contract = (((1,), (1,)), ((), ()))
    grad_hidden = lax.dot_general(
        grad_whole, down_weight, contract, preferred_element_type=jnp.float32
    )
    grad_gate = (
        grad_hidden * up_out * sigmoid_gate * (1.0 + gate_out * (1.0 - sigmoid_gate))
    ).astype(jnp.bfloat16)
    grad_up = (grad_hidden * activated).astype(jnp.bfloat16)
    back = lax.dot_general(grad_gate, gate_weight, contract, preferred_element_type=jnp.float32)
    back = back + lax.dot_general(grad_up, up_weight, contract, preferred_element_type=jnp.float32)
    back = lax.optimization_barrier(back.astype(jnp.bfloat16)).astype(jnp.float32)
    grad_normed = narrow(back)
    return grad_out.astype(jnp.float32) + norm_back(stream.astype(jnp.float32), gain * grad_normed)


def dense_body(
    token_ids, next_ids, embed_table, norm_gain, w_gate, w_up, w_down, mtp_gain, main_cot, mtp_cot
):
    sections = lax.axis_size("section")
    replicas = lax.axis_size("dp")
    section_index = lax.axis_index("section")
    replica = lax.axis_index("dp")
    mp_index = lax.axis_index("mp")
    batches = token_ids.shape[0]
    row_count = token_ids.shape[1] // replicas
    model_width = norm_gain.shape[1]
    vocab_rows = embed_table.shape[0]
    piece_width = embed_table.shape[1]
    is_first = section_index == 0
    is_last = section_index == sections - 1
    gain = norm_gain[0]
    gate_weight = w_gate[0]
    up_weight = w_up[0]
    down_weight = w_down[0]
    main_ids = token_ids.reshape(batches, replicas, row_count).transpose(1, 0, 2)
    after_ids = next_ids.reshape(batches, replicas, row_count).transpose(1, 0, 2)
    layout_ids = jnp.full((sections, replicas, batches, row_count), -1, jnp.int32)
    layout_ids = layout_ids.at[0].set(main_ids).at[sections - 1].set(after_ids)
    block_ids = layout_ids.reshape(-1)
    local_ids = block_ids - (section_index * replicas + replica) * vocab_rows
    inside = (local_ids >= 0) & (local_ids < vocab_rows)
    safe_ids = jnp.clip(local_ids, 0, vocab_rows - 1)
    picked = jnp.where(
        inside[:, None], jnp.take(embed_table, safe_ids, axis=0), jnp.zeros((), jnp.bfloat16)
    )
    own_piece = lax.psum_scatter(
        picked.astype(jnp.float32).astype(jnp.bfloat16),
        ("section", "dp"),
        scatter_dimension=0,
        tiled=True,
    ).astype(jnp.float32)
    own_piece = own_piece.astype(jnp.bfloat16).reshape(batches, row_count, piece_width)
    block_rows, main_full, mtp_full = (
        lax.all_gather(own_piece, "mp", axis=2, tiled=True),
        lax.all_gather(main_cot, "mp", axis=2, tiled=True),
        lax.all_gather(mtp_cot, "mp", axis=2, tiled=True),
    )
    local_rows = block_rows.shape[1]
    empty_rows = jnp.zeros((local_rows, model_width), jnp.bfloat16)
    empty_stack = jnp.zeros((batches, local_rows, model_width), jnp.bfloat16)
    ticks = batches + sections - 1

    def forward_tick(step_index, state_now):
        received, saved = state_now
        micro = step_index - section_index
        slot_index = jnp.clip(micro, 0, batches - 1)
        raw_rows = jnp.where(is_first, block_rows[slot_index], received)
        mixed = mixed_inputs(raw_rows, block_rows[slot_index], mtp_gain)
        block_in = jnp.where(is_last, mixed, raw_rows)
        result = forward_block(block_in, gain, gate_weight, up_weight, down_weight)
        active = (micro >= 0) & (micro < batches)
        saved = jnp.where(
            active, lax.dynamic_update_index_in_dim(saved, raw_rows, slot_index, 0), saved
        )
        return (send_down(result), saved)

    received, saved = lax.fori_loop(0, ticks, forward_tick, (empty_rows, empty_stack))

    def backward_tick(step_index, state_now):
        received, grads = state_now
        micro = step_index - (sections - 1 - section_index)
        slot_index = jnp.clip(micro, 0, batches - 1)
        raw_rows = saved[slot_index]
        embedded = block_rows[slot_index]
        mixed = mixed_inputs(raw_rows, embedded, mtp_gain)
        block_in = jnp.where(is_last, mixed, raw_rows)
        grad_out = jnp.where(is_last, mtp_full[slot_index], received)
        grad_in = backward_block(block_in, grad_out, gain, gate_weight, up_weight, down_weight)
        grad_main = main_full[slot_index].astype(jnp.float32) + norm_back(
            raw_rows.astype(jnp.float32), mtp_gain[0] * grad_in
        )
        grad_next = norm_back(embedded.astype(jnp.float32), mtp_gain[1] * grad_in)
        outgoing = jnp.where(is_last, grad_main, grad_in).astype(jnp.bfloat16)
        keeping = jnp.where(is_last, grad_next, grad_in).astype(jnp.bfloat16)
        active = (micro >= 0) & (micro < batches)
        grads = jnp.where(
            active, lax.dynamic_update_index_in_dim(grads, keeping, slot_index, 0), grads
        )
        return (send_up(outgoing), grads)

    received, grads = lax.fori_loop(0, ticks, backward_tick, (empty_rows, empty_stack))
    home = jnp.where(is_first | is_last, grads, jnp.zeros((), jnp.bfloat16))
    own_cols = lax.dynamic_slice_in_dim(home, mp_index * piece_width, piece_width, 2)
    everyone = lax.all_gather(
        own_cols.reshape(-1, piece_width), ("section", "dp"), axis=0, tiled=True
    )
    masked = jnp.where(inside[:, None], everyone.astype(jnp.float32), 0.0)
    table = jax.ops.segment_sum(masked, safe_ids, num_segments=vocab_rows)
    return table.astype(jnp.bfloat16)


MESH = pl.DeviceIdType.MESH
SLOTS = 16
BF = jnp.bfloat16
F32 = jnp.float32
COLS = (((1,), (1,)), ((), ()))


def dot(a, b):
    return jnp.dot(a, b, preferred_element_type=F32)


def dot_t(a, b):
    return lax.dot_general(a, b, COLS, preferred_element_type=F32)


def iota(shape, axis):
    return lax.broadcasted_iota(jnp.int32, shape, axis)


def loop(count, one):
    def step(index, carry):
        one(index)
        return carry

    lax.fori_loop(0, count, step, 0)


def remote(source, target, send_sem, recv_sem, device):
    return pltpu.make_async_remote_copy(
        src_ref=source,
        dst_ref=target,
        send_sem=send_sem,
        recv_sem=recv_sem,
        device_id=device,
        device_id_type=MESH,
    )


def to_column(row):
    count = row.shape[1]
    eye = iota((count, count), 0) == iota((count, count), 1)
    whole = jnp.broadcast_to(row, (count, count))
    return jnp.sum(jnp.where(eye, whole, jnp.zeros_like(whole)), axis=1, keepdims=True)


def to_row(column):
    count = column.shape[0]
    eye = iota((count, count), 0) == iota((count, count), 1)
    whole = jnp.broadcast_to(column, (count, count))
    return jnp.sum(jnp.where(eye, whole, jnp.zeros_like(whole)), axis=0, keepdims=True)


def total(values):
    return jnp.sum(values, axis=1, keepdims=True)


def step_kernel(
    sections,
    replicas,
    parts,
    ids_ref,
    main_cot_ref,
    mtp_cot_ref,
    gain_ref,
    mtp_gain_ref,
    table_hbm,
    gate_hbm,
    up_hbm,
    down_hbm,
    sums_ref,
    lid_ref,
    over_ref,
    table,
    first,
    rank,
    lid,
    onehot,
    send,
    recv,
    rows_ref,
    grad_ref,
    gu,
    down,
    relay_gu,
    relay_down,
    part_out,
    part_in,
    early_out,
    early_in,
    narrow_in,
    wide_in,
    stat_in,
    cross,
    hold,
    table_sem,
    local_sem,
    row_send,
    row_recv,
    sum_send,
    sum_recv,
    weight_local,
    weight_send,
    weight_recv,
    relay_send,
    relay_recv,
    part_send,
    part_recv,
    early_send,
    early_recv,
    wide_send,
    wide_recv,
    narrow_send,
    narrow_recv,
    stat_send,
    stat_recv,
    cross_send,
    cross_recv,
):
    section = lax.axis_index("section")
    replica = lax.axis_index("dp")
    part = lax.axis_index("mp")
    count = sections * replicas
    me = section * replicas + replica
    vocab_rows, width = table_hbm.shape
    hidden = gate_hbm.shape[1]
    tokens = ids_ref.shape[1]
    model_width = parts * width
    slots = count * SLOTS
    ring = parts // 2
    load = pltpu.make_async_copy(table_hbm, table, table_sem)
    load.start()

    def column_peer(step):
        there = step // replicas
        other = lax.rem(replica + 1 + step, replicas)
        return there * replicas + other, (there, other, part)

    def away(ahead, across):
        return lax.rem(part // 2 + ahead, ring) * 2 + lax.rem(part + across, 2)

    def row_peer(step):
        ahead = jnp.where(
            step < 2,
            1 + step * (ring - 2),
            jnp.where(step == 2, 0, jnp.where(step < 5, 1 + (step - 3) * (ring - 2), 2)),
        )
        across = jnp.where(step < 2, 0, jnp.where(step < 5, 1, step - 5))
        other = away(ahead, across)
        return other, (section, replica, other)

    barrier = pltpu.get_barrier_semaphore()

    def greet_column(step):
        other, device = column_peer(step)

        @pl.when(other != me)
        def _():
            pl.semaphore_signal(barrier, inc=1, device_id=device, device_id_type=MESH)

    def greet_row(step):
        other = lax.rem(part + 1 + lax.rem(step, parts - 1), parts)
        there = jnp.where(step < parts - 1, section, 1 - section)
        pl.semaphore_signal(
            barrier, inc=1, device_id=(there, replica, other), device_id_type=MESH
        )

    loop(count, greet_column)
    loop(2 * (parts - 1), greet_row)
    pl.semaphore_wait(barrier, count - 1 + 2 * (parts - 1))

    def weight_source(target):
        features = pl.ds(pl.multiple_of(target * width, width), width)
        return gate_hbm.at[features, :], up_hbm.at[features, :], down_hbm.at[:, features]

    def weight_slot(origin):
        return (
            gu.at[:, pl.ds(pl.multiple_of(origin * 2 * hidden, hidden), hidden)],
            gu.at[:, pl.ds(pl.multiple_of(origin * 2 * hidden + hidden, hidden), hidden)],
            down.at[pl.ds(pl.multiple_of(origin * hidden, hidden), hidden), :],
        )

    def relay_slot(way):
        return (
            relay_gu.at[way, :, pl.ds(0, hidden)],
            relay_gu.at[way, :, pl.ds(hidden, hidden)],
            relay_down.at[way],
        )

    def direct_copy(kind, step):
        other, device = row_peer(step)
        return remote(
            weight_source(other)[kind],
            weight_slot(part)[kind],
            weight_send.at[kind, step],
            weight_recv.at[kind, part],
            device,
        )

    def relay_copy(kind, way):
        final = away(2, way)
        return remote(
            weight_source(final)[kind],
            relay_slot(way)[kind],
            weight_send.at[kind, parts - 3 + way],
            relay_recv.at[kind, way],
            (section, replica, away(1 + way * (ring - 2), 0)),
        )

    def forward_copy(kind, way):
        origin = away(ring - 1 - way * (ring - 2), 0)
        final = away(1 + way * (ring - 2), way)
        return remote(
            relay_slot(way)[kind],
            weight_slot(origin)[kind],
            relay_send.at[kind, way],
            weight_recv.at[kind, origin],
            (section, replica, final),
        )

    def own_weight(kind):
        return pltpu.make_async_copy(
            weight_source(part)[kind], weight_slot(part)[kind], weight_local.at[kind]
        )

    def weights_start():
        for kind in range(3):
            for way in range(2):
                relay_copy(kind, way).start()
            loop(parts - 3, lambda step: direct_copy(kind, step).start())
        for kind in range(3):
            own_weight(kind).start()

    def relay_on(kinds):
        for kind in kinds:
            for way in range(2):
                relay_copy(kind, way).wait_recv()
                forward_copy(kind, way).start()

    def weight_wait(kind, step):
        other, device = row_peer(step)
        remote(
            weight_slot(other)[kind],
            weight_slot(other)[kind],
            weight_send.at[kind, step],
            weight_recv.at[kind, other],
            device,
        ).wait_recv()

    @pl.when(section == 0)
    def _():
        weights_start()

    earlier = iota((tokens, tokens), 0) < iota((tokens, tokens), 1)

    def find_first(step):
        for inner in range(4):
            index = pl.ds(step * 4 + inner, 1)
            row = ids_ref[index, :]
            same = (to_column(row) == row) & earlier
            seen = jnp.max(jnp.where(same, 1.0, 0.0), axis=0, keepdims=True)
            first[index, :] = 1.0 - seen

    loop(count // 4, find_first)
    shard = ids_ref[...] // vocab_rows
    mine = jnp.where(shard == me, first[...], 0.0)
    triangle = jnp.where(earlier, 1.0, 0.0).astype(BF)
    rank[...] = jnp.where(mine > 0.0, dot(mine.astype(BF), triangle), -1.0)

    def find_lid(step):
        for inner in range(4):
            index = step * 4 + inner
            row = ids_ref[pl.ds(index, 1), :] - me * vocab_rows + 1
            picks = rank[pl.ds(index, 1), :].astype(jnp.int32) == iota((SLOTS, tokens), 0)
            found = jnp.sum(
                jnp.where(picks, jnp.broadcast_to(row, picks.shape), 0), axis=1, keepdims=True
            )
            lid[pl.ds(pl.multiple_of(index * SLOTS, SLOTS), SLOTS), :] = jnp.broadcast_to(
                found - 1, (SLOTS, tokens)
            )

    loop(count // 4, find_lid)
    load.wait()

    def row_copy(step):
        other, device = column_peer(step)
        return remote(send.at[other], recv.at[me], row_send.at[step], row_recv.at[me], device)

    for half in range(sections):

        def mark(step):
            other = column_peer(half * replicas + step)[0]
            wanted = lid[pl.ds(pl.multiple_of(other * SLOTS, SLOTS), SLOTS), :]
            place = pl.ds(pl.multiple_of(step * SLOTS, SLOTS), SLOTS)
            for lane in range(vocab_rows // tokens):
                hit = wanted == iota(wanted.shape, 1) + lane * tokens
                onehot[place, pl.ds(lane * tokens, tokens)] = jnp.where(hit, 1.0, 0.0).astype(BF)

        loop(replicas, mark)
        found = dot(onehot[...], table[...]).astype(BF)
        for step in range(replicas):
            here = half * replicas + step
            other = column_peer(here)[0]
            send[other] = found[step * SLOTS : (step + 1) * SLOTS]

        def go(step):
            here = half * replicas + step

            @pl.when(column_peer(here)[0] != me)
            def _():
                row_copy(here).start()

        loop(replicas, go)
    recv[me] = send[me]

    @pl.when(section == 1)
    def _():
        weights_start()

    relay_on((0, 1))

    def fill(index, most):
        held = jnp.where(shard == index, first[...], 0.0)
        return jnp.maximum(most, total(held))

    most = lax.fori_loop(0, count, fill, jnp.zeros((count, 1), F32))
    over_ref[...] = jnp.broadcast_to(jnp.max(most, axis=0, keepdims=True), over_ref.shape)
    eye = iota((tokens, tokens), 0) == iota((tokens, tokens), 1)
    for block in range(slots // tokens):
        rows = pl.ds(block * tokens, tokens)
        row = jnp.sum(jnp.where(eye, lid[rows, :], 0), axis=0, keepdims=True)
        lid_ref[:, rows] = jnp.broadcast_to(row, (8, tokens))
    own_row = ids_ref[pl.ds(me, 1), :]
    own_first = first[pl.ds(me, 1), :]
    own_column = to_column(own_row)
    shard_row = own_row // vocab_rows
    counted = (own_column // vocab_rows == shard_row) & earlier & (to_column(own_first) > 0.0)
    slot_row = shard_row * SLOTS + jnp.sum(jnp.where(counted, 1, 0), axis=0, keepdims=True)
    leads = (own_column == own_row) & (own_first > 0.0)
    slot_column = total(jnp.where(leads, jnp.broadcast_to(slot_row, leads.shape), 0))

    def row_wait(step):
        other, device = column_peer(step)

        @pl.when(other != me)
        def _():
            remote(
                send.at[me], recv.at[other], row_send.at[step], row_recv.at[other], device
            ).wait_recv()

    loop(count, row_wait)
    spread = jnp.where(slot_column == iota((tokens, slots), 1), 1.0, 0.0).astype(BF)
    rows_ref[...] = dot(spread, recv[...].reshape(slots, width)).astype(BF)

    features = pl.ds(pl.multiple_of(part * width, width), width)
    gain = gain_ref[0:1, features]
    gain_main = mtp_gain_ref[0:1, features]
    gain_next = mtp_gain_ref[1:2, features]

    def inverse(sum_of_squares):
        return lax.rsqrt(sum_of_squares / model_width + EPS)

    def lanes(index, size):
        return pl.ds(pl.multiple_of(index * size, size), size)

    def put_stats(slot, columns):
        rows = [to_row(column) for column in columns]
        rows = rows + [jnp.zeros_like(rows[0])] * (8 - len(rows))
        stat_in[slot, part] = jnp.concatenate(rows, axis=0)

    def get_stats(slot, number):
        value = stat_in[slot, 0]
        for index in range(1, parts):
            value = value + stat_in[slot, index]
        return [to_column(value[index : index + 1, :]) for index in range(number)]

    def stat_copy(slot, step):
        return remote(
            stat_in.at[slot, part],
            stat_in.at[slot, part],
            stat_send.at[slot, step],
            stat_recv.at[slot, part],
            row_peer(step)[1],
        )

    def share_stats(slot):
        loop(parts - 1, lambda step: stat_copy(slot, step).start())

    def wait_stats(slot):
        def one(step):
            other, device = row_peer(step)
            remote(
                stat_in.at[slot, other],
                stat_in.at[slot, other],
                stat_send.at[slot, step],
                stat_recv.at[slot, other],
                device,
            ).wait()

        loop(parts - 1, one)

    def tell_copy(step):
        other = lax.rem(part + step, parts)
        return remote(
            stat_in.at[1, part],
            stat_in.at[1, part],
            stat_send.at[1, step],
            stat_recv.at[1, part],
            (1 - section, replica, other),
        )

    def gate_up_start(normed):
        def partial(other):
            part_out[other] = dot(normed, gu[:, lanes(other, 2 * hidden)]).astype(BF)

        def one(step):
            other, device = row_peer(step)
            weight_wait(0, step)
            weight_wait(1, step)
            partial(other)
            remote(
                part_out.at[other],
                part_in.at[part],
                part_send.at[step],
                part_recv.at[part],
                device,
            ).start()

        loop(parts - 1, one)
        own_weight(0).wait()
        own_weight(1).wait()
        partial(part)

    def gate_up_wait():
        def one(step, value):
            other, device = row_peer(step)
            remote(
                part_in.at[other],
                part_in.at[other],
                part_send.at[step],
                part_recv.at[other],
                device,
            ).wait()
            return value + part_in[other].astype(F32)

        return lax.fori_loop(0, parts - 1, one, part_out[part].astype(F32))

    def down_wait():
        loop(parts - 1, lambda step: weight_wait(2, step))
        own_weight(2).wait()

    def grad_hidden_start(grad):
        early_out[...] = dot_t(grad, down[...]).astype(BF)

        def one(step):
            other, device = row_peer(step)
            remote(
                early_out.at[:, lanes(other, hidden)],
                early_in.at[part],
                early_send.at[step],
                early_recv.at[part],
                device,
            ).start()

        loop(parts - 1, one)

    def grad_hidden_wait():
        def one(step, value):
            other, device = row_peer(step)
            remote(
                early_in.at[other],
                early_in.at[other],
                early_send.at[step],
                early_recv.at[other],
                device,
            ).wait()
            return value + early_in[other].astype(F32)

        return lax.fori_loop(
            0, parts - 1, one, early_out[:, lanes(part, hidden)].astype(F32)
        )

    def share_columns(whole, size, send_sem, recv_sem):
        def start(step):
            device = row_peer(step)[1]
            own = whole.at[:, lanes(part, size)]
            remote(own, own, send_sem.at[step], recv_sem.at[part], device).start()

        def wait(step):
            other, device = row_peer(step)
            theirs = whole.at[:, lanes(other, size)]
            remote(theirs, theirs, send_sem.at[step], recv_sem.at[other], device).wait()

        loop(parts - 1, start)
        loop(parts - 1, wait)

    def backward(gate, up, grad_hidden):
        sigmoid = jax.nn.sigmoid(gate)
        grad_gate = grad_hidden * up * sigmoid * (1.0 + gate * (1.0 - sigmoid))
        grad_up = grad_hidden * gate * sigmoid
        wide_in[:, lanes(part, 2 * hidden)] = jnp.concatenate(
            [grad_gate, grad_up], axis=1
        ).astype(BF)
        share_columns(wide_in, 2 * hidden, wide_send, wide_recv)
        return dot_t(wide_in[...], gu[...]) * gain

    over = remote(
        cross.at[0], cross.at[1], cross_send, cross_recv, (1 - section, replica, part)
    )

    @pl.when(section == 0)
    def _():
        rows = rows_ref[...].astype(F32)
        put_stats(0, [total(rows * rows)])
        share_stats(0)
        gate_up_start((rows * gain).astype(BF))
        relay_on((2,))
        wait_stats(0)
        scale = inverse(get_stats(0, 1)[0])
        whole = gate_up_wait() * scale
        hold[...] = whole
        gate = whole[:, :hidden]
        up = whole[:, hidden:]
        narrow_in[:, lanes(part, hidden)] = (gate * jax.nn.sigmoid(gate) * up).astype(BF)
        share_columns(narrow_in, hidden, narrow_send, narrow_recv)
        down_wait()
        out = rows_ref[...].astype(F32) + dot(narrow_in[...], down[...])
        cross[0] = out.astype(BF)
        over.start()
        main = cross[0].astype(F32)
        put_stats(1, [total(main * main)])
        loop(parts, lambda step: tell_copy(step).start())
        loop(parts, lambda step: tell_copy(step).wait_send())
        over.wait()
        grad = cross[1]
        grad_hidden_start(grad)
        grad_hidden = grad_hidden_wait()
        whole = hold[...]
        scaled = backward(whole[:, :hidden], whole[:, hidden:], grad_hidden)
        rows = rows_ref[...].astype(F32)
        put_stats(2, [total(rows * scaled)])
        share_stats(2)
        wait_stats(2)
        mean = get_stats(2, 1)[0] / model_width
        scale = inverse(get_stats(0, 1)[0])
        result = grad.astype(F32) + scale * scaled - rows * (scale * scale * scale * mean)
        grad_ref[...] = result.astype(BF)

    @pl.when(section == 1)
    def _():
        rows = rows_ref[...].astype(F32)
        put_stats(0, [total(rows * rows)])
        share_stats(0)
        relay_on((2,))
        wait_stats(0)
        scale_next = inverse(get_stats(0, 1)[0])
        down_wait()
        grad_hidden_start(mtp_cot_ref[...])
        grad_hidden = grad_hidden_wait()

        def heard(index):
            remote(
                stat_in.at[1, index],
                stat_in.at[1, index],
                stat_send.at[1, 0],
                stat_recv.at[1, index],
                (1 - section, replica, part),
            ).wait_recv()

        loop(parts, heard)
        over.wait_recv()
        scale_main = inverse(get_stats(1, 1)[0])
        main = cross[1].astype(F32)
        mixed = (main * scale_main * gain_main + rows * scale_next * gain_next).astype(BF)
        mixed = mixed.astype(F32)
        put_stats(2, [total(mixed * mixed)])
        share_stats(2)
        gate_up_start((mixed * gain).astype(BF))
        wait_stats(2)
        scale = inverse(get_stats(2, 1)[0])
        whole = gate_up_wait() * scale
        scaled = backward(whole[:, :hidden], whole[:, hidden:], grad_hidden)
        cot = mtp_cot_ref[...].astype(F32)
        next_weighted = rows * gain_next
        main_weighted = main * gain_main
        put_stats(
            3,
            [
                total(mixed * scaled),
                total(next_weighted * scaled),
                total(next_weighted * mixed),
                total(next_weighted * cot),
                total(main_weighted * scaled),
                total(main_weighted * mixed),
                total(main_weighted * cot),
            ],
        )
        share_stats(3)
        wait_stats(3)
        s1, s2, s3, s4, s5, s6, s7 = get_stats(3, 7)
        slope = scale * scale * scale * (s1 / model_width)
        grad_mixed = cot + scale * scaled - mixed * slope
        mean_next = (s4 + scale * s2 - slope * s3) / model_width
        mean_main = (s7 + scale * s5 - slope * s6) / model_width
        grad_main = (
            main_cot_ref[...].astype(F32)
            + scale_main * (gain_main * grad_mixed)
            - main * (scale_main * scale_main * scale_main * mean_main)
        )
        cross[0] = grad_main.astype(BF)
        over.start()
        grad_next = scale_next * (gain_next * grad_mixed) - rows * (
            scale_next * scale_next * scale_next * mean_next
        )
        grad_ref[...] = grad_next.astype(BF)
        over.wait_send()

    def row_done(step):
        @pl.when(column_peer(step)[0] != me)
        def _():
            row_copy(step).wait_send()

    loop(count, row_done)
    back = jnp.where(to_row(slot_column) == iota((slots, tokens), 0), 1.0, 0.0).astype(BF)
    send[...] = dot(back, grad_ref[...]).astype(BF).reshape(count, SLOTS, width)

    def sum_copy(step):
        other, device = column_peer(step)
        return remote(
            send.at[other], sums_ref.at[me], sum_send.at[step], sum_recv.at[me], device
        )

    def sum_start(step):
        @pl.when(column_peer(step)[0] != me)
        def _():
            sum_copy(step).start()

    loop(count, sum_start)
    sums_ref[me] = send[me]

    for kind in range(3):
        for way in range(2):
            relay_copy(kind, way).wait_send()
            forward_copy(kind, way).wait_send()
        loop(parts - 3, lambda step: direct_copy(kind, step).wait_send())

    def sum_wait(step):
        other, device = column_peer(step)

        @pl.when(other != me)
        def _():
            remote(
                send.at[other],
                sums_ref.at[other],
                sum_send.at[step],
                sum_recv.at[other],
                device,
            ).wait()

    loop(count, sum_wait)


def place_kernel(lid_ref, sums_ref, out_ref):
    rows = out_ref.shape[0]
    slots = sums_ref.shape[0]
    base = pl.program_id(0) * rows
    hit = lid_ref[0:1, :] == iota((rows, slots), 0) + base
    out_ref[...] = dot(jnp.where(hit, 1.0, 0.0).astype(BF), sums_ref[...]).astype(BF)


def vmem():
    return pl.BlockSpec(memory_space=pltpu.VMEM)


def anywhere():
    return pl.BlockSpec(memory_space=pl.ANY)


def dma(*shape):
    return pltpu.SemaphoreType.DMA(shape)


def fast_body(
    token_ids, next_ids, embed_table, norm_gain, w_gate, w_up, w_down, mtp_gain, main_cot, mtp_cot
):
    sections = lax.axis_size("section")
    replicas = lax.axis_size("dp")
    parts = lax.axis_size("mp")
    count = sections * replicas
    batches = token_ids.shape[0]
    row_count = token_ids.shape[1] // replicas
    tokens = batches * row_count
    vocab_rows, width = embed_table.shape
    hidden = w_gate.shape[2]
    ids = jnp.stack([token_ids, next_ids]).reshape(sections, batches, replicas, row_count)
    ids = ids.transpose(0, 2, 1, 3).reshape(count, tokens)
    slots = count * SLOTS
    sums, lid_row, most = pl.pallas_call(
        functools.partial(step_kernel, sections, replicas, parts),
        out_shape=(
            jax.ShapeDtypeStruct((count, SLOTS, width), BF),
            jax.ShapeDtypeStruct((8, slots), jnp.int32),
            jax.ShapeDtypeStruct((8, 128), F32),
        ),
        in_specs=[vmem()] * 5 + [anywhere()] * 4,
        out_specs=(vmem(), vmem(), vmem()),
        scratch_shapes=[
            pltpu.VMEM((vocab_rows, width), BF),
            pltpu.VMEM((count, tokens), F32),
            pltpu.VMEM((count, tokens), F32),
            pltpu.VMEM((slots, tokens), jnp.int32),
            pltpu.VMEM((replicas * SLOTS, vocab_rows), BF),
            pltpu.VMEM((count, SLOTS, width), BF),
            pltpu.VMEM((count, SLOTS, width), BF),
            pltpu.VMEM((tokens, width), BF),
            pltpu.VMEM((tokens, width), BF),
            pltpu.VMEM((width, parts * 2 * hidden), BF),
            pltpu.VMEM((parts * hidden, width), BF),
            pltpu.VMEM((2, width, 2 * hidden), BF),
            pltpu.VMEM((2, hidden, width), BF),
            pltpu.VMEM((parts, tokens, 2 * hidden), BF),
            pltpu.VMEM((parts, tokens, 2 * hidden), BF),
            pltpu.VMEM((tokens, parts * hidden), BF),
            pltpu.VMEM((parts, tokens, hidden), BF),
            pltpu.VMEM((tokens, parts * hidden), BF),
            pltpu.VMEM((tokens, parts * 2 * hidden), BF),
            pltpu.VMEM((4, parts, 8, tokens), F32),
            pltpu.VMEM((2, tokens, width), BF),
            pltpu.VMEM((tokens, 2 * hidden), F32),
            pltpu.SemaphoreType.DMA,
            pltpu.SemaphoreType.DMA,
            dma(count),
            dma(count),
            dma(count),
            dma(count),
            dma(3),
            dma(3, parts),
            dma(3, parts),
            dma(3, 2),
            dma(3, 2),
            dma(parts),
            dma(parts),
            dma(parts),
            dma(parts),
            dma(parts),
            dma(parts),
            dma(parts),
            dma(parts),
            dma(4, parts),
            dma(4, parts),
            pltpu.SemaphoreType.DMA,
            pltpu.SemaphoreType.DMA,
        ],
        compiler_params=pltpu.CompilerParams(
            collective_id=0, has_side_effects=True, vmem_limit_bytes=56 << 20
        ),
        name="train_step",
    )(
        ids,
        main_cot.reshape(tokens, width),
        mtp_cot.reshape(tokens, width),
        norm_gain,
        mtp_gain,
        embed_table,
        w_gate[0],
        w_up[0],
        w_down[0],
    )
    return most[0, 0], lid_row, sums.reshape(slots, width)


def place(lid_row, sums, vocab_rows):
    slots, width = sums.shape
    block = vocab_rows // 8
    return pl.pallas_call(
        place_kernel,
        grid=(vocab_rows // block,),
        out_shape=jax.ShapeDtypeStruct((vocab_rows, width), BF),
        in_specs=[
            pl.BlockSpec((8, slots), lambda i: (0, 0)),
            pl.BlockSpec((slots, width), lambda i: (0, 0)),
        ],
        out_specs=pl.BlockSpec((block, width), lambda i: (i, 0)),
        name="place_rows",
    )(lid_row, sums)


def body(*arguments):
    most, lid_row, sums = fast_body(*arguments)
    vocab_rows = arguments[2].shape[0]
    return lax.cond(
        most <= SLOTS,
        lambda *given: place(given[0], given[1], vocab_rows),
        lambda *given: dense_body(*given[2:]),
        lid_row,
        sums,
        *arguments,
    )


def solution(mesh):
    return jax.shard_map(
        body,
        mesh=mesh,
        in_specs=(
            P(),
            P(),
            P(("section", "dp"), "mp"),
            P("section", None),
            P("section", None, "mp"),
            P("section", None, "mp"),
            P("section", "mp", None),
            P(),
            P(None, "dp", "mp"),
            P(None, "dp", "mp"),
        ),
        out_specs=P(("section", "dp"), "mp"),
        check_vma=False,
    )
```

```python
import functools

import jax
import jax.numpy as jnp
from jax import lax
from jax.experimental import pallas as pl
from jax.experimental.pallas import tpu as pltpu
from jax.sharding import PartitionSpec as P

EPS = 1e-06
MESH = pl.DeviceIdType.MESH
FEW_SLOTS = 16
BF = jnp.bfloat16
F32 = jnp.float32
COLS = (((1,), (1,)), ((), ()))


def dot(a, b):
    return jnp.dot(a, b, preferred_element_type=F32)


def dot_t(a, b):
    return lax.dot_general(a, b, COLS, preferred_element_type=F32)


def iota(shape, axis):
    return lax.broadcasted_iota(jnp.int32, shape, axis)


def loop(count, one):
    def step(index, carry):
        one(index)
        return carry

    lax.fori_loop(0, count, step, 0)


def remote(source, target, send_sem, recv_sem, device):
    return pltpu.make_async_remote_copy(
        src_ref=source,
        dst_ref=target,
        send_sem=send_sem,
        recv_sem=recv_sem,
        device_id=device,
        device_id_type=MESH,
    )


def to_column(row):
    count = row.shape[1]
    eye = iota((count, count), 0) == iota((count, count), 1)
    whole = jnp.broadcast_to(row, (count, count))
    return jnp.sum(jnp.where(eye, whole, jnp.zeros_like(whole)), axis=1, keepdims=True)


def to_row(column):
    count = column.shape[0]
    eye = iota((count, count), 0) == iota((count, count), 1)
    whole = jnp.broadcast_to(column, (count, count))
    return jnp.sum(jnp.where(eye, whole, jnp.zeros_like(whole)), axis=0, keepdims=True)


def total(values):
    return jnp.sum(values, axis=1, keepdims=True)


def step_kernel(
    sections,
    replicas,
    parts,
    per_pair,
    token_ids_ref,
    next_ids_ref,
    main_cot_ref,
    mtp_cot_ref,
    gain_ref,
    mtp_gain_ref,
    table_hbm,
    gate_hbm,
    up_hbm,
    down_hbm,
    sums_ref,
    lid_ref,
    over_ref,
    table,
    ids_ref,
    first,
    rank,
    lid,
    onehot,
    send,
    recv,
    rows_ref,
    grad_ref,
    gu,
    down,
    relay_gu,
    relay_down,
    part_out,
    part_in,
    early_out,
    early_in,
    narrow_in,
    wide_in,
    stat_in,
    mixed_all,
    cot_all,
    back_out,
    back_in,
    back_relay,
    cross,
    hold,
    table_sem,
    local_sem,
    row_send,
    row_recv,
    sum_send,
    sum_recv,
    weight_local,
    local_weight,
    weight_send,
    weight_recv,
    relay_send,
    relay_recv,
    part_send,
    part_recv,
    early_send,
    early_recv,
    wide_send,
    wide_recv,
    narrow_send,
    narrow_recv,
    stat_send,
    stat_recv,
    cross_send,
    cross_recv,
    mixed_send,
    mixed_recv,
    cot_send,
    cot_recv,
    back_send,
    back_recv,
    back_relay_send,
    back_relay_recv,
):
    section = lax.axis_index("section")
    replica = lax.axis_index("dp")
    part = lax.axis_index("mp")
    count = sections * replicas
    me = section * replicas + replica
    vocab_rows, width = table_hbm.shape
    hidden = gate_hbm.shape[1]
    batches = token_ids_ref.shape[0]
    tokens = ids_ref.shape[1]
    run = tokens // batches
    model_width = parts * width
    slots = count * per_pair
    ring = parts // 2
    load = pltpu.make_async_copy(table_hbm, table, table_sem)
    load.start()

    def column_peer(step):
        there = step // replicas
        other = lax.rem(replica + 1 + step, replicas)
        return there * replicas + other, (there, other, part)

    def away(ahead, across):
        return lax.rem(part // 2 + ahead, ring) * 2 + lax.rem(part + across, 2)

    def row_peer(step):
        ahead = jnp.where(
            step < 2,
            1 + step * (ring - 2),
            jnp.where(step == 2, 0, jnp.where(step < 5, 1 + (step - 3) * (ring - 2), 2)),
        )
        across = jnp.where(step < 2, 0, jnp.where(step < 5, 1, step - 5))
        other = away(ahead, across)
        return other, (section, replica, other)

    barrier = pltpu.get_barrier_semaphore()

    def greet_column(step):
        other, device = column_peer(step)

        @pl.when(other != me)
        def _():
            pl.semaphore_signal(barrier, inc=1, device_id=device, device_id_type=MESH)

    def greet_row(step):
        other = lax.rem(part + 1 + lax.rem(step, parts - 1), parts)
        there = jnp.where(step < parts - 1, section, 1 - section)
        pl.semaphore_signal(
            barrier, inc=1, device_id=(there, replica, other), device_id_type=MESH
        )

    loop(count, greet_column)
    loop(2 * (parts - 1), greet_row)

    rows_of = 2 * batches
    row_index = lax.rem(iota((rows_of, tokens), 0), batches)
    own_run = iota((rows_of, tokens), 1) // run == row_index
    for group in range(replicas // batches):
        columns = pl.ds(group * tokens, tokens)
        both = jnp.concatenate(
            [token_ids_ref[:, columns], next_ids_ref[:, columns]], axis=0
        ).astype(F32)
        turned = [both] + [pltpu.roll(both, shift * run, 1) for shift in range(1, batches)]
        for inner in range(batches):
            value = jnp.zeros_like(both)
            for shift in range(batches):
                wanted = own_run & (lax.rem(row_index - inner + batches, batches) == shift)
                value = jnp.where(wanted, turned[shift], value)
            index = group * batches + inner
            ids_ref[index : index + 1, :] = jnp.sum(value[:batches], axis=0, keepdims=True)
            ids_ref[replicas + index : replicas + index + 1, :] = jnp.sum(
                value[batches:], axis=0, keepdims=True
            )

    earlier = iota((tokens, tokens), 0) < iota((tokens, tokens), 1)

    def find_first(step):
        for inner in range(4):
            index = pl.ds(step * 4 + inner, 1)
            row = ids_ref[index, :]
            same = (to_column(row) == row) & earlier
            seen = jnp.max(jnp.where(same, 1.0, 0.0), axis=0, keepdims=True)
            first[index, :] = 1.0 - seen

    loop(replicas // 4, find_first)
    pl.semaphore_wait(barrier, count - 1 + 2 * (parts - 1))

    def weight_source(target):
        features = pl.ds(pl.multiple_of(target * width, width), width)
        return gate_hbm.at[features, :], up_hbm.at[features, :], down_hbm.at[:, features]

    def weight_slot(origin):
        return (
            gu.at[origin, :, pl.ds(0, hidden)],
            gu.at[origin, :, pl.ds(hidden, hidden)],
            down.at[origin],
        )

    def relay_slot(way):
        return (
            relay_gu.at[way, :, pl.ds(0, hidden)],
            relay_gu.at[way, :, pl.ds(hidden, hidden)],
            relay_down.at[way],
        )

    def direct_copy(kind, step):
        other, device = row_peer(step)
        return remote(
            weight_source(other)[kind],
            weight_slot(part)[kind],
            weight_send.at[kind, step],
            weight_recv.at[kind, part],
            device,
        )

    def relay_copy(kind, way):
        final = away(2, way)
        return remote(
            weight_source(final)[kind],
            relay_slot(way)[kind],
            weight_send.at[kind, parts - 3 + way],
            relay_recv.at[kind, way],
            (section, replica, away(1 + way * (ring - 2), 0)),
        )

    def forward_copy(kind, way):
        origin = away(ring - 1 - way * (ring - 2), 0)
        final = away(1 + way * (ring - 2), way)
        return remote(
            relay_slot(way)[kind],
            weight_slot(origin)[kind],
            relay_send.at[kind, way],
            weight_recv.at[kind, origin],
            (section, replica, final),
        )

    def own_weight(kind):
        return pltpu.make_async_copy(
            weight_source(part)[kind], weight_slot(part)[kind], weight_local.at[kind]
        )

    def local_weights(then):
        def one(target):
            for kind, source in enumerate(weight_source(target)):
                then(
                    pltpu.make_async_copy(
                        source, weight_slot(target)[kind], local_weight.at[kind, target]
                    )
                )

        loop(parts, one)

    def weights_start():
        for kind in range(3):
            for way in range(2):
                relay_copy(kind, way).start()
            loop(parts - 3, lambda step: direct_copy(kind, step).start())
        for kind in range(3):
            own_weight(kind).start()

    def relay_on(kinds):
        for kind in kinds:
            for way in range(2):
                relay_copy(kind, way).wait_recv()
                forward_copy(kind, way).start()

    def weight_wait(kind, step):
        other, device = row_peer(step)
        remote(
            weight_slot(other)[kind],
            weight_slot(other)[kind],
            weight_send.at[kind, step],
            weight_recv.at[kind, other],
            device,
        ).wait_recv()

    @pl.when(section == 0)
    def _():
        weights_start()

    @pl.when(section == 1)
    def _():
        local_weights(lambda copy: copy.start())

    def shard_of(rows):
        return jnp.floor(rows * (1.0 / vocab_rows))

    triangle = jnp.where(earlier, 1.0, 0.0).astype(BF)
    me_f = me.astype(F32)
    group = min(replicas, max(1, 2 * tokens // per_pair))

    def row_copy(step):
        other, device = column_peer(step)
        return remote(send.at[other], recv.at[me], row_send.at[step], row_recv.at[me], device)

    def send_rows(half):
        half_rows = pl.ds(half * replicas, replicas)
        mine = jnp.where(shard_of(ids_ref[half_rows, :]) == me_f, first[half_rows, :], 0.0)
        rank[...] = jnp.where(mine > 0.0, dot(mine.astype(BF), triangle), -1.0)

        def find_lid(step):
            for inner in range(4):
                index = step * 4 + inner
                there = half * replicas + index
                row = ids_ref[pl.ds(there, 1), :] - (me_f * vocab_rows - 1.0)
                picks = rank[pl.ds(index, 1), :].astype(jnp.int32) == iota(
                    (per_pair, tokens), 0
                )
                found = total(jnp.where(picks, jnp.broadcast_to(row, picks.shape), 0.0))
                lid[pl.ds(pl.multiple_of(there * per_pair, per_pair), per_pair), :] = (
                    jnp.broadcast_to(found - 1.0, (per_pair, tokens)).astype(jnp.int32)
                )

        loop(replicas // 4, find_lid)

        def chunk(block):
            base = half * replicas + block * group

            def mark(step):
                other = column_peer(base + step)[0]
                wanted = lid[
                    pl.ds(pl.multiple_of(other * per_pair, per_pair), per_pair), :
                ]
                there = pl.ds(pl.multiple_of(step * per_pair, per_pair), per_pair)
                for lane in range(vocab_rows // tokens):
                    hit = wanted == iota(wanted.shape, 1) + lane * tokens
                    onehot[there, pl.ds(lane * tokens, tokens)] = jnp.where(
                        hit, 1.0, 0.0
                    ).astype(BF)

            loop(group, mark)
            found = dot(onehot[...], table[...]).astype(BF)
            for step in range(group):
                other = column_peer(base + step)[0]
                send[other] = found[step * per_pair : (step + 1) * per_pair]

            def go(step):
                @pl.when(column_peer(base + step)[0] != me)
                def _():
                    row_copy(base + step).start()

            loop(group, go)

        if group == replicas:
            chunk(0)
        else:
            loop(replicas // group, chunk)

    load.wait()
    send_rows(0)
    loop(replicas // 4, lambda step: find_first(step + replicas // 4))
    send_rows(1)
    recv[me] = send[me]

    @pl.when(section == 0)
    def _():
        relay_on((0, 1))

    shard = shard_of(ids_ref[...])

    def fill(step, most):
        for inner in range(4):
            held = jnp.where(shard == (step * 4 + inner).astype(F32), first[...], 0.0)
            most = jnp.maximum(most, total(held))
        return most

    most = lax.fori_loop(0, count // 4, fill, jnp.zeros((count, 1), F32))
    over_ref[...] = jnp.broadcast_to(jnp.max(most, axis=0, keepdims=True), over_ref.shape)
    eye = iota((tokens, tokens), 0) == iota((tokens, tokens), 1)

    def turn(block):
        rows = pl.ds(pl.multiple_of(block * tokens, tokens), tokens)
        row = jnp.sum(jnp.where(eye, lid[rows, :], 0), axis=0, keepdims=True)
        lid_ref[:, rows] = jnp.broadcast_to(row, (8, tokens))

    loop(slots // tokens, turn)
    own_row = ids_ref[pl.ds(me, 1), :]
    own_first = first[pl.ds(me, 1), :]
    own_column = to_column(own_row)
    shard_row = shard_of(own_row)
    counted = (shard_of(own_column) == shard_row) & earlier & (to_column(own_first) > 0.0)
    slot_row = shard_row * per_pair + jnp.sum(
        jnp.where(counted, 1.0, 0.0), axis=0, keepdims=True
    )
    leads = (own_column == own_row) & (own_first > 0.0)
    slot_column = total(jnp.where(leads, jnp.broadcast_to(slot_row, leads.shape), 0.0))

    def row_wait(step):
        other, device = column_peer(step)

        @pl.when(other != me)
        def _():
            remote(
                send.at[me], recv.at[other], row_send.at[step], row_recv.at[other], device
            ).wait_recv()

    loop(count, row_wait)
    slot_of = slot_column.astype(jnp.int32)
    spread = jnp.where(slot_of == iota((tokens, slots), 1), 1.0, 0.0).astype(BF)
    rows_ref[...] = dot(spread, recv[...].reshape(slots, width)).astype(BF)

    features = pl.ds(pl.multiple_of(part * width, width), width)
    gain = gain_ref[0:1, features]
    gain_main = mtp_gain_ref[0:1, features]
    gain_next = mtp_gain_ref[1:2, features]

    def inverse(sum_of_squares):
        return lax.rsqrt(sum_of_squares / model_width + EPS)

    def lanes(index, size):
        return pl.ds(pl.multiple_of(index * size, size), size)

    def put_stats(slot, columns):
        rows = [to_row(column) for column in columns]
        rows = rows + [jnp.zeros_like(rows[0])] * (8 - len(rows))
        stat_in[slot, part] = jnp.concatenate(rows, axis=0)

    def get_stats(slot, number):
        value = stat_in[slot, 0]
        for index in range(1, parts):
            value = value + stat_in[slot, index]
        return [to_column(value[index : index + 1, :]) for index in range(number)]

    def stat_copy(slot, step):
        return remote(
            stat_in.at[slot, part],
            stat_in.at[slot, part],
            stat_send.at[slot, step],
            stat_recv.at[slot, part],
            row_peer(step)[1],
        )

    def share_stats(slot):
        loop(parts - 1, lambda step: stat_copy(slot, step).start())

    def wait_stats(slot):
        def one(step):
            other, device = row_peer(step)
            remote(
                stat_in.at[slot, other],
                stat_in.at[slot, other],
                stat_send.at[slot, step],
                stat_recv.at[slot, other],
                device,
            ).wait()

        loop(parts - 1, one)

    def tell_copy(step):
        other = lax.rem(part + step, parts)
        return remote(
            stat_in.at[1, part],
            stat_in.at[1, part],
            stat_send.at[1, step],
            stat_recv.at[1, part],
            (1 - section, replica, other),
        )

    def gate_up_start(normed):
        def partial(other):
            part_out[other] = dot(normed, gu[other]).astype(BF)

        def one(step):
            other, device = row_peer(step)
            weight_wait(0, step)
            weight_wait(1, step)
            partial(other)
            remote(
                part_out.at[other],
                part_in.at[part],
                part_send.at[step],
                part_recv.at[part],
                device,
            ).start()

        loop(parts - 1, one)
        own_weight(0).wait()
        own_weight(1).wait()
        partial(part)

    def gate_up_wait():
        def one(step, value):
            other, device = row_peer(step)
            remote(
                part_in.at[other],
                part_in.at[other],
                part_send.at[step],
                part_recv.at[other],
                device,
            ).wait()
            return value + part_in[other].astype(F32)

        return lax.fori_loop(0, parts - 1, one, part_out[part].astype(F32))

    def down_wait():
        loop(parts - 1, lambda step: weight_wait(2, step))
        own_weight(2).wait()

    def grad_hidden_start(grad):
        early_out[...] = dot_t(grad, down[...].reshape(parts * hidden, width)).astype(BF)

        def one(step):
            other, device = row_peer(step)
            remote(
                early_out.at[:, lanes(other, hidden)],
                early_in.at[part],
                early_send.at[step],
                early_recv.at[part],
                device,
            ).start()

        loop(parts - 1, one)

    def grad_hidden_wait():
        def one(step, value):
            other, device = row_peer(step)
            remote(
                early_in.at[other],
                early_in.at[other],
                early_send.at[step],
                early_recv.at[other],
                device,
            ).wait()
            return value + early_in[other].astype(F32)

        return lax.fori_loop(
            0, parts - 1, one, early_out[:, lanes(part, hidden)].astype(F32)
        )

    def share_columns(whole, size, send_sem, recv_sem):
        def start(step):
            device = row_peer(step)[1]
            own = whole.at[:, lanes(part, size)]
            remote(own, own, send_sem.at[step], recv_sem.at[part], device).start()

        def wait(step):
            other, device = row_peer(step)
            theirs = whole.at[:, lanes(other, size)]
            remote(theirs, theirs, send_sem.at[step], recv_sem.at[other], device).wait()

        loop(parts - 1, start)
        loop(parts - 1, wait)

    def slopes(gate, up, grad_hidden):
        sigmoid = jax.nn.sigmoid(gate)
        grad_gate = grad_hidden * up * sigmoid * (1.0 + gate * (1.0 - sigmoid))
        grad_up = grad_hidden * gate * sigmoid
        return jnp.concatenate([grad_gate, grad_up], axis=1).astype(BF)

    def block_copy(whole, send_sem, recv_sem, block, step, device):
        return remote(
            whole.at[block], whole.at[block], send_sem.at[step], recv_sem.at[block], device
        )

    def gather_blocks(whole, send_sem, recv_sem, use):
        up_one = (section, replica, away(1, 0))
        down_one = (section, replica, away(ring - 1, 0))
        beside = (section, replica, away(0, 1))
        plan = [
            (away(0, 0), (up_one, down_one, beside)),
            (away(0, 1), (up_one, down_one)),
            (away(ring - 1, 0), (up_one,)),
            (away(1, 0), ()),
            (away(1, 1), (down_one,)),
            (away(ring - 1, 1), ()),
            (away(2, 0), ()),
            (away(2, 1), ()),
        ]
        step = 0
        sent = []
        for position, (block, devices) in enumerate(plan):
            if position > 0:
                block_copy(whole, send_sem, recv_sem, block, 0, beside).wait_recv()
            for device in devices:
                copy = block_copy(whole, send_sem, recv_sem, block, step, device)
                copy.start()
                sent.append(copy)
                step += 1
            use(block)
        for copy in sent:
            copy.wait_send()

    def gather_dot(whole, send_sem, recv_sem, product):
        held = []

        def use(block):
            held.append(product(whole[block], block))

        gather_blocks(whole, send_sem, recv_sem, use)
        value = held[0]
        for other in held[1:]:
            value = value + other
        return value

    def return_blocks(terms):
        up_one = (section, replica, away(1, 0))
        down_one = (section, replica, away(ring - 1, 0))
        plan = [
            (away(2, 0), up_one, 0),
            (away(2, 1), down_one, 1),
            (away(1, 1), None, None),
            (away(ring - 1, 1), None, None),
            (away(1, 0), None, None),
            (away(ring - 1, 0), None, None),
            (away(0, 1), None, None),
        ]
        sent = []
        for step, (block, device, way) in enumerate(plan):
            back_out[block] = dot_t(terms, gu[block]).astype(BF)
            target = back_in.at[part] if way is None else back_relay.at[way]
            arrived = back_recv.at[part] if way is None else back_relay_recv.at[way]
            copy = remote(
                back_out.at[block],
                target,
                back_send.at[step],
                arrived,
                (section, replica, block) if device is None else device,
            )
            copy.start()
            sent.append(copy)
        own = dot_t(terms, gu[part])
        for way in range(2):
            origin = away(ring - 1 - way * (ring - 2), 0)
            final = away(1 + way * (ring - 2), way)
            sent[way].wait_recv()
            copy = remote(
                back_relay.at[way],
                back_in.at[origin],
                back_relay_send.at[way],
                back_recv.at[origin],
                (section, replica, final),
            )
            copy.start()
            sent.append(copy)
        for block in (
            away(0, 1),
            away(1, 0),
            away(ring - 1, 0),
            away(1, 1),
            away(ring - 1, 1),
            away(2, 0),
            away(2, 1),
        ):
            remote(
                back_in.at[block],
                back_in.at[block],
                back_send.at[0],
                back_recv.at[block],
                (section, replica, block),
            ).wait_recv()
            own = own + back_in[block].astype(F32)
        for copy in sent:
            copy.wait_send()
        return own * gain

    over = remote(
        cross.at[0], cross.at[1], cross_send, cross_recv, (1 - section, replica, part)
    )

    @pl.when(section == 0)
    def _():
        rows = rows_ref[...].astype(F32)
        put_stats(0, [total(rows * rows)])
        share_stats(0)
        gate_up_start((rows * gain).astype(BF))
        relay_on((2,))
        wait_stats(0)
        scale = inverse(get_stats(0, 1)[0])
        whole = gate_up_wait() * scale
        hold[...] = whole
        gate = whole[:, :hidden]
        up = whole[:, hidden:]
        narrow_in[:, lanes(part, hidden)] = (gate * jax.nn.sigmoid(gate) * up).astype(BF)
        share_columns(narrow_in, hidden, narrow_send, narrow_recv)
        down_wait()
        out = rows_ref[...].astype(F32) + dot(narrow_in[...], down[...].reshape(parts * hidden, width))
        cross[0] = out.astype(BF)
        over.start()
        main = cross[0].astype(F32)
        put_stats(1, [total(main * main)])
        loop(parts, lambda step: tell_copy(step).start())
        loop(parts, lambda step: tell_copy(step).wait_send())
        over.wait()
        grad = cross[1]
        grad_hidden_start(grad)
        grad_hidden = grad_hidden_wait()
        whole = hold[...]
        wide_in[:, lanes(part, 2 * hidden)] = slopes(
            whole[:, :hidden], whole[:, hidden:], grad_hidden
        )
        share_columns(wide_in, 2 * hidden, wide_send, wide_recv)
        scaled = dot_t(wide_in[:, pl.ds(0, 2 * hidden)], gu[0])
        for index in range(1, parts):
            scaled = scaled + dot_t(
                wide_in[:, pl.ds(index * 2 * hidden, 2 * hidden)], gu[index]
            )
        scaled = scaled * gain
        rows = rows_ref[...].astype(F32)
        put_stats(2, [total(rows * scaled)])
        share_stats(2)
        wait_stats(2)
        mean = get_stats(2, 1)[0] / model_width
        scale = inverse(get_stats(0, 1)[0])
        result = grad.astype(F32) + scale * scaled - rows * (scale * scale * scale * mean)
        grad_ref[...] = result.astype(BF)

    @pl.when(section == 1)
    def _():
        rows = rows_ref[...].astype(F32)
        put_stats(0, [total(rows * rows)])
        share_stats(0)
        local_weights(lambda copy: copy.wait())
        cot_all[part] = mtp_cot_ref[...]
        grad_hidden = gather_dot(
            cot_all, cot_send, cot_recv, lambda block, index: dot_t(block, down[index])
        )
        wait_stats(0)
        scale_next = inverse(get_stats(0, 1)[0])

        def heard(index):
            remote(
                stat_in.at[1, index],
                stat_in.at[1, index],
                stat_send.at[1, 0],
                stat_recv.at[1, index],
                (1 - section, replica, part),
            ).wait_recv()

        loop(parts, heard)
        over.wait_recv()
        scale_main = inverse(get_stats(1, 1)[0])
        main = cross[1].astype(F32)
        mixed = (main * scale_main * gain_main + rows * scale_next * gain_next).astype(BF)
        mixed = mixed.astype(F32)
        put_stats(2, [total(mixed * mixed)])
        share_stats(2)
        mixed_all[part] = (mixed * gain).astype(BF)
        whole = gather_dot(
            mixed_all, mixed_send, mixed_recv, lambda block, index: dot(block, gu[index])
        )
        wait_stats(2)
        scale = inverse(get_stats(2, 1)[0])
        whole = whole * scale
        scaled = return_blocks(slopes(whole[:, :hidden], whole[:, hidden:], grad_hidden))
        cot = mtp_cot_ref[...].astype(F32)
        next_weighted = rows * gain_next
        main_weighted = main * gain_main
        put_stats(
            3,
            [
                total(mixed * scaled),
                total(next_weighted * scaled),
                total(next_weighted * mixed),
                total(next_weighted * cot),
                total(main_weighted * scaled),
                total(main_weighted * mixed),
                total(main_weighted * cot),
            ],
        )
        share_stats(3)
        wait_stats(3)
        s1, s2, s3, s4, s5, s6, s7 = get_stats(3, 7)
        slope = scale * scale * scale * (s1 / model_width)
        grad_mixed = cot + scale * scaled - mixed * slope
        mean_next = (s4 + scale * s2 - slope * s3) / model_width
        mean_main = (s7 + scale * s5 - slope * s6) / model_width
        grad_main = (
            main_cot_ref[...].astype(F32)
            + scale_main * (gain_main * grad_mixed)
            - main * (scale_main * scale_main * scale_main * mean_main)
        )
        cross[0] = grad_main.astype(BF)
        over.start()
        grad_next = scale_next * (gain_next * grad_mixed) - rows * (
            scale_next * scale_next * scale_next * mean_next
        )
        grad_ref[...] = grad_next.astype(BF)
        over.wait_send()

    def row_done(step):
        @pl.when(column_peer(step)[0] != me)
        def _():
            row_copy(step).wait_send()

    loop(count, row_done)
    slot_back = to_row(slot_column).astype(jnp.int32)
    group_rows = group * per_pair

    def pack(block):
        hit = slot_back == iota((group_rows, tokens), 0) + block * group_rows
        found = dot(jnp.where(hit, 1.0, 0.0).astype(BF), grad_ref[...]).astype(BF)
        send[pl.ds(block * group, group)] = found.reshape(group, per_pair, width)

    loop(count // group, pack)

    def sum_copy(step):
        other, device = column_peer(step)
        return remote(
            send.at[other], sums_ref.at[me], sum_send.at[step], sum_recv.at[me], device
        )

    def sum_start(step):
        @pl.when(column_peer(step)[0] != me)
        def _():
            sum_copy(step).start()

    loop(count, sum_start)
    sums_ref[me] = send[me]

    @pl.when(section == 0)
    def _():
        for kind in range(3):
            for way in range(2):
                relay_copy(kind, way).wait_send()
                forward_copy(kind, way).wait_send()
            loop(parts - 3, lambda step: direct_copy(kind, step).wait_send())

    def sum_wait(step):
        other, device = column_peer(step)

        @pl.when(other != me)
        def _():
            remote(
                send.at[other],
                sums_ref.at[other],
                sum_send.at[step],
                sum_recv.at[other],
                device,
            ).wait()

    loop(count, sum_wait)


def place_kernel(lid_ref, sums_ref, out_ref):
    rows = out_ref.shape[0]
    slots = sums_ref.shape[0]
    base = pl.program_id(0) * rows
    hit = lid_ref[0:1, :] == iota((rows, slots), 0) + base
    out_ref[...] = dot(jnp.where(hit, 1.0, 0.0).astype(BF), sums_ref[...]).astype(BF)


def vmem():
    return pl.BlockSpec(memory_space=pltpu.VMEM)


def anywhere():
    return pl.BlockSpec(memory_space=pl.ANY)


def dma(*shape):
    return pltpu.SemaphoreType.DMA(shape)


def train_step(
    per_pair,
    token_ids,
    next_ids,
    embed_table,
    norm_gain,
    w_gate,
    w_up,
    w_down,
    mtp_gain,
    main_cot,
    mtp_cot,
):
    sections = lax.axis_size("section")
    replicas = lax.axis_size("dp")
    parts = lax.axis_size("mp")
    count = sections * replicas
    batches = token_ids.shape[0]
    tokens = batches * (token_ids.shape[1] // replicas)
    vocab_rows, width = embed_table.shape
    hidden = w_gate.shape[2]
    slots = count * per_pair
    picked = min(replicas * per_pair, max(2 * tokens, per_pair))
    block = pltpu.VMEM((parts, tokens, width), BF)
    one = pltpu.SemaphoreType.DMA
    return pl.pallas_call(
        functools.partial(step_kernel, sections, replicas, parts, per_pair),
        out_shape=(
            jax.ShapeDtypeStruct((count, per_pair, width), BF),
            jax.ShapeDtypeStruct((8, slots), jnp.int32),
            jax.ShapeDtypeStruct((8, 128), F32),
        ),
        in_specs=[vmem()] * 6 + [anywhere()] * 4,
        out_specs=(vmem(), vmem(), vmem()),
        scratch_shapes=[
            pltpu.VMEM((vocab_rows, width), BF),
            pltpu.VMEM((count, tokens), F32),
            pltpu.VMEM((count, tokens), F32),
            pltpu.VMEM((replicas, tokens), F32),
            pltpu.VMEM((slots, tokens), jnp.int32),
            pltpu.VMEM((picked, vocab_rows), BF),
            pltpu.VMEM((count, per_pair, width), BF),
            pltpu.VMEM((count, per_pair, width), BF),
            pltpu.VMEM((tokens, width), BF),
            pltpu.VMEM((tokens, width), BF),
            pltpu.VMEM((parts, width, 2 * hidden), BF),
            pltpu.VMEM((parts, hidden, width), BF),
            pltpu.VMEM((2, width, 2 * hidden), BF),
            pltpu.VMEM((2, hidden, width), BF),
            pltpu.VMEM((parts, tokens, 2 * hidden), BF),
            pltpu.VMEM((parts, tokens, 2 * hidden), BF),
            pltpu.VMEM((tokens, parts * hidden), BF),
            pltpu.VMEM((parts, tokens, hidden), BF),
            pltpu.VMEM((tokens, parts * hidden), BF),
            pltpu.VMEM((tokens, parts * 2 * hidden), BF),
            pltpu.VMEM((4, parts, 8, tokens), F32),
            block,
            block,
            block,
            block,
            pltpu.VMEM((2, tokens, width), BF),
            pltpu.VMEM((2, tokens, width), BF),
            pltpu.VMEM((tokens, 2 * hidden), F32),
            one,
            one,
            dma(count),
            dma(count),
            dma(count),
            dma(count),
            dma(3),
            dma(3, parts),
            dma(3, parts),
            dma(3, parts),
            dma(3, 2),
            dma(3, 2),
        ]
        + [dma(parts)] * 8
        + [dma(4, parts)] * 2
        + [one] * 2
        + [dma(parts)] * 6
        + [dma(2)] * 2,
        compiler_params=pltpu.CompilerParams(
            collective_id=0 if per_pair == FEW_SLOTS else 1,
            has_side_effects=True,
            vmem_limit_bytes=60 << 20,
        ),
        name=f"train_step_{per_pair}",
    )(
        token_ids,
        next_ids,
        main_cot.reshape(tokens, width),
        mtp_cot.reshape(tokens, width),
        norm_gain,
        mtp_gain,
        embed_table,
        w_gate[0],
        w_up[0],
        w_down[0],
    )


def place(lid_row, sums, vocab_rows):
    width = sums.shape[-1]
    slots = lid_row.shape[1]
    block = vocab_rows // 8
    return pl.pallas_call(
        place_kernel,
        grid=(vocab_rows // block,),
        out_shape=jax.ShapeDtypeStruct((vocab_rows, width), BF),
        in_specs=[
            pl.BlockSpec((8, slots), lambda i: (0, 0)),
            pl.BlockSpec((slots, width), lambda i: (0, 0)),
        ],
        out_specs=pl.BlockSpec((block, width), lambda i: (i, 0)),
        compiler_params=pltpu.CompilerParams(vmem_limit_bytes=56 << 20),
        name="place_rows",
    )(lid_row, sums.reshape(slots, width))


def body(*arguments):
    vocab_rows = arguments[2].shape[0]
    positions = arguments[0].shape[0] * (arguments[0].shape[1] // lax.axis_size("dp"))
    sums, lid_row, most = train_step(FEW_SLOTS, *arguments)

    def few(sums, lid_row, *given):
        return place(lid_row, sums, vocab_rows)

    def many(sums, lid_row, *given):
        sums, lid_row, most = train_step(positions, *given)
        return place(lid_row, sums, vocab_rows)

    return lax.cond(most[0, 0] <= FEW_SLOTS, few, many, sums, lid_row, *arguments)


def solution(mesh):
    return jax.shard_map(
        body,
        mesh=mesh,
        in_specs=(
            P(),
            P(),
            P(("section", "dp"), "mp"),
            P("section", None),
            P("section", None, "mp"),
            P("section", None, "mp"),
            P("section", "mp", None),
            P(),
            P(None, "dp", "mp"),
            P(None, "dp", "mp"),
        ),
        out_specs=P(("section", "dp"), "mp"),
        check_vma=False,
    )
```

```python
import functools

import jax
import jax.numpy as jnp
from jax import lax
from jax.experimental import pallas as pl
from jax.experimental.pallas import tpu as pltpu
from jax.sharding import PartitionSpec as P

EPS = 1e-06
MESH = pl.DeviceIdType.MESH
FEW_SLOTS = 32
BF = jnp.bfloat16
F32 = jnp.float32
COLS = (((1,), (1,)), ((), ()))


def dot(a, b):
    return jnp.dot(a, b, preferred_element_type=F32)


def dot_t(a, b):
    return lax.dot_general(a, b, COLS, preferred_element_type=F32)


def iota(shape, axis):
    return lax.broadcasted_iota(jnp.int32, shape, axis)


def loop(count, one):
    def step(index, carry):
        one(index)
        return carry

    lax.fori_loop(0, count, step, 0)


def remote(source, target, send_sem, recv_sem, device):
    return pltpu.make_async_remote_copy(
        src_ref=source,
        dst_ref=target,
        send_sem=send_sem,
        recv_sem=recv_sem,
        device_id=device,
        device_id_type=MESH,
    )


def to_column(row):
    count = row.shape[1]
    eye = iota((count, count), 0) == iota((count, count), 1)
    whole = jnp.broadcast_to(row, (count, count))
    return jnp.sum(jnp.where(eye, whole, jnp.zeros_like(whole)), axis=1, keepdims=True)


def to_row(column):
    count = column.shape[0]
    eye = iota((count, count), 0) == iota((count, count), 1)
    whole = jnp.broadcast_to(column, (count, count))
    return jnp.sum(jnp.where(eye, whole, jnp.zeros_like(whole)), axis=0, keepdims=True)


def total(values):
    return jnp.sum(values, axis=1, keepdims=True)


def step_kernel(
    sections,
    replicas,
    parts,
    per_pair,
    token_ids_ref,
    next_ids_ref,
    main_cot_ref,
    mtp_cot_ref,
    gain_ref,
    mtp_gain_ref,
    table_hbm,
    gate_hbm,
    up_hbm,
    down_hbm,
    sums_ref,
    lid_ref,
    over_ref,
    table,
    ids_ref,
    first,
    rank,
    lid,
    onehot,
    send,
    swap_out,
    swap_in,
    recv,
    rows_ref,
    grad_ref,
    gu,
    down,
    relay_gu,
    relay_down,
    part_out,
    part_in,
    early_out,
    early_in,
    narrow_in,
    wide_in,
    stat_in,
    mixed_all,
    cot_all,
    back_out,
    back_in,
    back_relay,
    cross,
    hold,
    table_sem,
    local_sem,
    swap_send,
    swap_recv,
    row_send,
    row_recv,
    sum_send,
    sum_recv,
    pass_send,
    pass_recv,
    weight_local,
    local_weight,
    weight_send,
    weight_recv,
    relay_send,
    relay_recv,
    part_send,
    part_recv,
    early_send,
    early_recv,
    wide_send,
    wide_recv,
    narrow_send,
    narrow_recv,
    stat_send,
    stat_recv,
    cross_send,
    cross_recv,
    mixed_send,
    mixed_recv,
    cot_send,
    cot_recv,
    back_send,
    back_recv,
    back_relay_send,
    back_relay_recv,
):
    section = lax.axis_index("section")
    replica = lax.axis_index("dp")
    part = lax.axis_index("mp")
    count = sections * replicas
    me = section * replicas + replica
    vocab_rows, width = table_hbm.shape
    hidden = gate_hbm.shape[1]
    batches = token_ids_ref.shape[0]
    tokens = ids_ref.shape[1]
    run = tokens // batches
    model_width = parts * width
    half = per_pair // 2
    slots = replicas * per_pair
    ring = parts // 2
    load = pltpu.make_async_copy(table_hbm, table, table_sem)
    load.start()

    def column_peer(step):
        other = lax.rem(replica + 1 + step, replicas)
        return other, (section, other, part)

    partner = (1 - section, replica, part)

    def away(ahead, across):
        return lax.rem(part // 2 + ahead, ring) * 2 + lax.rem(part + across, 2)

    def row_peer(step):
        ahead = jnp.where(
            step < 2,
            1 + step * (ring - 2),
            jnp.where(step == 2, 0, jnp.where(step < 5, 1 + (step - 3) * (ring - 2), 2)),
        )
        across = jnp.where(step < 2, 0, jnp.where(step < 5, 1, step - 5))
        other = away(ahead, across)
        return other, (section, replica, other)

    barrier = pltpu.get_barrier_semaphore()

    def greet_column(step):
        device = column_peer(step)[1]
        pl.semaphore_signal(barrier, inc=1, device_id=device, device_id_type=MESH)

    def greet_row(step):
        other = lax.rem(part + 1 + lax.rem(step, parts), parts)
        there = jnp.where(step < parts - 1, section, 1 - section)
        other = jnp.where(step < parts - 1, other, lax.rem(part + step, parts))
        pl.semaphore_signal(
            barrier, inc=1, device_id=(there, replica, other), device_id_type=MESH
        )

    loop(replicas - 1, greet_column)
    loop(2 * parts - 1, greet_row)

    rows_of = 2 * batches
    row_index = lax.rem(iota((rows_of, tokens), 0), batches)
    own_run = iota((rows_of, tokens), 1) // run == row_index
    for group in range(replicas // batches):
        columns = pl.ds(group * tokens, tokens)
        both = jnp.concatenate(
            [token_ids_ref[:, columns], next_ids_ref[:, columns]], axis=0
        ).astype(F32)
        turned = [both] + [pltpu.roll(both, shift * run, 1) for shift in range(1, batches)]
        for inner in range(batches):
            value = jnp.zeros_like(both)
            for shift in range(batches):
                wanted = own_run & (lax.rem(row_index - inner + batches, batches) == shift)
                value = jnp.where(wanted, turned[shift], value)
            index = group * batches + inner
            ids_ref[index : index + 1, :] = jnp.sum(value[:batches], axis=0, keepdims=True)
            ids_ref[replicas + index : replicas + index + 1, :] = jnp.sum(
                value[batches:], axis=0, keepdims=True
            )

    earlier = iota((tokens, tokens), 0) < iota((tokens, tokens), 1)

    def find_first(step):
        for inner in range(4):
            index = pl.ds(step * 4 + inner, 1)
            row = ids_ref[index, :]
            same = (to_column(row) == row) & earlier
            seen = jnp.max(jnp.where(same, 1.0, 0.0), axis=0, keepdims=True)
            first[index, :] = 1.0 - seen

    loop(count // 4, find_first)
    pl.semaphore_wait(barrier, replicas - 1 + 2 * parts - 1)

    def weight_source(target):
        features = pl.ds(pl.multiple_of(target * width, width), width)
        return gate_hbm.at[features, :], up_hbm.at[features, :], down_hbm.at[:, features]

    def weight_slot(origin):
        return (
            gu.at[origin, :, pl.ds(0, hidden)],
            gu.at[origin, :, pl.ds(hidden, hidden)],
            down.at[origin],
        )

    def relay_slot(way):
        return (
            relay_gu.at[way, :, pl.ds(0, hidden)],
            relay_gu.at[way, :, pl.ds(hidden, hidden)],
            relay_down.at[way],
        )

    def direct_copy(kind, step):
        other, device = row_peer(step)
        return remote(
            weight_source(other)[kind],
            weight_slot(part)[kind],
            weight_send.at[kind, step],
            weight_recv.at[kind, part],
            device,
        )

    def relay_copy(kind, way):
        final = away(2, way)
        return remote(
            weight_source(final)[kind],
            relay_slot(way)[kind],
            weight_send.at[kind, parts - 3 + way],
            relay_recv.at[kind, way],
            (section, replica, away(1 + way * (ring - 2), 0)),
        )

    def forward_copy(kind, way):
        origin = away(ring - 1 - way * (ring - 2), 0)
        final = away(1 + way * (ring - 2), way)
        return remote(
            relay_slot(way)[kind],
            weight_slot(origin)[kind],
            relay_send.at[kind, way],
            weight_recv.at[kind, origin],
            (section, replica, final),
        )

    def own_weight(kind):
        return pltpu.make_async_copy(
            weight_source(part)[kind], weight_slot(part)[kind], weight_local.at[kind]
        )

    def local_weights(then):
        def one(target):
            for kind, source in enumerate(weight_source(target)):
                then(
                    pltpu.make_async_copy(
                        source, weight_slot(target)[kind], local_weight.at[kind, target]
                    )
                )

        loop(parts, one)

    def weights_start():
        for kind in range(3):
            for way in range(2):
                relay_copy(kind, way).start()
            loop(parts - 3, lambda step: direct_copy(kind, step).start())
        for kind in range(3):
            own_weight(kind).start()

    def relay_on(kinds):
        for kind in kinds:
            for way in range(2):
                relay_copy(kind, way).wait_recv()
                forward_copy(kind, way).start()

    def weight_wait(kind, step):
        other, device = row_peer(step)
        remote(
            weight_slot(other)[kind],
            weight_slot(other)[kind],
            weight_send.at[kind, step],
            weight_recv.at[kind, other],
            device,
        ).wait_recv()

    @pl.when(section == 0)
    def _():
        weights_start()

    @pl.when(section == 1)
    def _():
        local_weights(lambda copy: copy.start())

    def shard_of(rows):
        return jnp.floor(rows * (1.0 / vocab_rows))

    def chip_of(rows):
        shards = shard_of(rows)
        return shards - replicas * jnp.floor(shards * (1.0 / replicas))

    triangle = jnp.where(earlier, 1.0, 0.0).astype(BF)
    me_f = me.astype(F32)
    here_f = replica.astype(F32)
    group = min(replicas, max(1, 2 * tokens // half))

    def row_copy(step):
        other, device = column_peer(step)
        return remote(
            send.at[other],
            recv.at[section, replica],
            row_send.at[step],
            row_recv.at[replica],
            device,
        )

    def ranks(first_row):
        rows = pl.ds(first_row, replicas)
        mine = jnp.where(chip_of(ids_ref[rows, :]) == here_f, first[rows, :], 0.0)
        return mine, dot(mine.astype(BF), triangle)

    mine, order = ranks(0)
    before = total(mine)
    rank[pl.ds(0, replicas), :] = jnp.where(mine > 0.0, order, -1.0)
    mine, order = ranks(replicas)
    rank[pl.ds(replicas, replicas), :] = jnp.where(mine > 0.0, order + before, -1.0)

    def find_lid(step):
        for inner in range(2):
            index = step * 2 + inner
            found = jnp.zeros((per_pair, 1), F32)
            for offset in (0, replicas):
                row = ids_ref[pl.ds(index + offset, 1), :] - (me_f * vocab_rows - 1.0)
                picks = rank[pl.ds(index + offset, 1), :].astype(jnp.int32) == iota(
                    (per_pair, tokens), 0
                )
                found += total(jnp.where(picks, jnp.broadcast_to(row, picks.shape), 0.0))
            whole = jnp.broadcast_to(found - 1.0, (per_pair, tokens)).astype(jnp.int32)
            for side in range(2):
                place = pl.multiple_of((side * replicas + index) * half, half)
                lid[pl.ds(place, half), :] = whole[side * half : (side + 1) * half]

    loop(replicas // 2, find_lid)

    def pick_rows(side, put):
        def chunk(block):
            base = block * group

            def mark(step):
                place = pl.multiple_of((side * replicas + base + step) * half, half)
                wanted = lid[pl.ds(place, half), :]
                there = pl.ds(pl.multiple_of(step * half, half), half)
                for lane in range(vocab_rows // tokens):
                    hit = wanted == iota(wanted.shape, 1) + lane * tokens
                    onehot[there, pl.ds(lane * tokens, tokens)] = jnp.where(
                        hit, 1.0, 0.0
                    ).astype(BF)

            loop(group, mark)
            found = dot(onehot[...], table[...]).astype(BF)
            put(pl.ds(base, group), found.reshape(group, half, width))

        if group == replicas:
            chunk(0)
        else:
            loop(replicas // group, chunk)

    def swap_copy(turn):
        return remote(
            swap_out, swap_in, swap_send.at[turn], swap_recv.at[turn], partner
        )

    def put_swap(place, values):
        swap_out[place] = values

    def put_send(place, values):
        send[place] = values

    load.wait()
    pick_rows(1 - section, put_swap)
    swap_copy(0).start()
    pick_rows(section, put_send)
    swap_copy(0).wait()
    send[...] = send[...] + swap_in[...]
    loop(replicas - 1, lambda step: row_copy(step).start())
    recv[section, replica] = send[replica]

    @pl.when(section == 0)
    def _():
        relay_on((0, 1, 2))

    chip = chip_of(ids_ref[...])

    def fill(step, most):
        for inner in range(4):
            held = jnp.where(chip == (step * 4 + inner).astype(F32), first[...], 0.0)
            held = total(held)
            most = jnp.maximum(most, held[:replicas] + held[replicas:])
        return most

    most = lax.fori_loop(0, replicas // 4, fill, jnp.zeros((replicas, 1), F32))
    over_ref[...] = jnp.broadcast_to(jnp.max(most, axis=0, keepdims=True), over_ref.shape)
    eye = iota((tokens, tokens), 0) == iota((tokens, tokens), 1)

    def turn(block):
        rows = pl.ds(pl.multiple_of(block * tokens, tokens), tokens)
        row = jnp.sum(jnp.where(eye, lid[rows, :], 0), axis=0, keepdims=True)
        lid_ref[:, rows] = jnp.broadcast_to(row, (8, tokens))

    loop(slots // tokens, turn)
    own_row = ids_ref[pl.ds(me, 1), :]
    own_first = first[pl.ds(me, 1), :]
    own_column = to_column(own_row)
    chip_row = chip_of(own_row)
    counted = (chip_of(own_column) == chip_row) & earlier & (to_column(own_first) > 0.0)
    main_chip = chip_of(to_column(ids_ref[pl.ds(replica, 1), :]))
    main_first = to_column(first[pl.ds(replica, 1), :])
    ahead = jnp.where((main_chip == chip_row) & (main_first > 0.0), 1.0, 0.0)
    rank_row = jnp.sum(
        jnp.where(counted, 1.0, 0.0) + ahead * section.astype(F32), axis=0, keepdims=True
    )
    side_row = jnp.floor(rank_row * (1.0 / half))
    slot_row = (side_row * (replicas - 1) + chip_row) * half + rank_row
    leads = (own_column == own_row) & (own_first > 0.0)
    slot_column = total(jnp.where(leads, jnp.broadcast_to(slot_row, leads.shape), 0.0))

    def pass_copy(whole, turn, block):
        return remote(
            whole.at[section, block],
            whole.at[section, block],
            pass_send.at[turn, block],
            pass_recv.at[turn, block],
            partner,
        )

    def collect(whole, turn, send_sem, recv_sem):
        pass_copy(whole, turn, replica).start()

        def arrive(step):
            other = lax.rem(replica + replicas - 1 - step, replicas)
            remote(
                whole.at[section, other],
                whole.at[section, other],
                send_sem.at[step],
                recv_sem.at[other],
                partner,
            ).wait_recv()
            pass_copy(whole, turn, other).start()

        def passed(block):
            remote(
                whole.at[1 - section, block],
                whole.at[1 - section, block],
                pass_send.at[turn, block],
                pass_recv.at[turn, block],
                partner,
            ).wait()

        loop(replicas - 1, arrive)
        loop(replicas, passed)

    def block_copy(whole, send_sem, recv_sem, block, step, device):
        return remote(
            whole.at[block], whole.at[block], send_sem.at[step], recv_sem.at[block], device
        )

    def gather_blocks(whole, send_sem, recv_sem, use):
        up_one = (section, replica, away(1, 0))
        down_one = (section, replica, away(ring - 1, 0))
        beside = (section, replica, away(0, 1))
        plan = [
            (away(0, 0), (up_one, down_one, beside)),
            (away(0, 1), (up_one, down_one)),
            (away(ring - 1, 0), (up_one,)),
            (away(1, 0), ()),
            (away(1, 1), (down_one,)),
            (away(ring - 1, 1), ()),
            (away(2, 0), ()),
            (away(2, 1), ()),
        ]
        step = 0
        sent = []
        for position, (block, devices) in enumerate(plan):
            if position > 0:
                block_copy(whole, send_sem, recv_sem, block, 0, beside).wait_recv()
            for device in devices:
                copy = block_copy(whole, send_sem, recv_sem, block, step, device)
                copy.start()
                sent.append(copy)
                step += 1
            use(block)
        for copy in sent:
            copy.wait_send()

    def gather_dot(whole, send_sem, recv_sem, product):
        held = []

        def use(block):
            held.append(product(whole[block], block))

        gather_blocks(whole, send_sem, recv_sem, use)
        value = held[0]
        for other in held[1:]:
            value = value + other
        return value

    collect(recv, 0, row_send, row_recv)
    slot_of = slot_column.astype(jnp.int32)
    spread = jnp.where(slot_of == iota((tokens, slots), 1), 1.0, 0.0).astype(BF)
    rows_ref[...] = dot(spread, recv[...].reshape(slots, width)).astype(BF)

    features = pl.ds(pl.multiple_of(part * width, width), width)
    gain = gain_ref[0:1, features]
    gain_main = mtp_gain_ref[0:1, features]
    gain_next = mtp_gain_ref[1:2, features]

    def inverse(sum_of_squares):
        return lax.rsqrt(sum_of_squares / model_width + EPS)

    def lanes(index, size):
        return pl.ds(pl.multiple_of(index * size, size), size)

    def put_stats(slot, columns):
        rows = [to_row(column) for column in columns]
        rows = rows + [jnp.zeros_like(rows[0])] * (8 - len(rows))
        stat_in[slot, part] = jnp.concatenate(rows, axis=0)

    def get_stats(slot, number):
        value = stat_in[slot, 0]
        for index in range(1, parts):
            value = value + stat_in[slot, index]
        return [to_column(value[index : index + 1, :]) for index in range(number)]

    def stat_copy(slot, step):
        return remote(
            stat_in.at[slot, part],
            stat_in.at[slot, part],
            stat_send.at[slot, step],
            stat_recv.at[slot, part],
            row_peer(step)[1],
        )

    def share_stats(slot):
        loop(parts - 1, lambda step: stat_copy(slot, step).start())

    def wait_stats(slot):
        def one(step):
            other, device = row_peer(step)
            remote(
                stat_in.at[slot, other],
                stat_in.at[slot, other],
                stat_send.at[slot, step],
                stat_recv.at[slot, other],
                device,
            ).wait()

        loop(parts - 1, one)

    def tell_copy(step):
        other = lax.rem(part + step, parts)
        return remote(
            stat_in.at[1, part],
            stat_in.at[1, part],
            stat_send.at[1, step],
            stat_recv.at[1, part],
            (1 - section, replica, other),
        )

    def gate_up_start(normed):
        def partial(other):
            part_out[other] = dot(normed, gu[other]).astype(BF)

        def one(step):
            other, device = row_peer(step)
            weight_wait(0, step)
            weight_wait(1, step)
            partial(other)
            remote(
                part_out.at[other],
                part_in.at[part],
                part_send.at[step],
                part_recv.at[part],
                device,
            ).start()

        loop(parts - 1, one)
        own_weight(0).wait()
        own_weight(1).wait()
        partial(part)

    def gate_up_wait():
        def one(step, value):
            other, device = row_peer(step)
            remote(
                part_in.at[other],
                part_in.at[other],
                part_send.at[step],
                part_recv.at[other],
                device,
            ).wait()
            return value + part_in[other].astype(F32)

        return lax.fori_loop(0, parts - 1, one, part_out[part].astype(F32))

    def down_wait():
        loop(parts - 1, lambda step: weight_wait(2, step))
        own_weight(2).wait()

    def grad_hidden_start(grad):
        early_out[...] = dot_t(grad, down[...].reshape(parts * hidden, width)).astype(BF)

        def one(step):
            other, device = row_peer(step)
            remote(
                early_out.at[:, lanes(other, hidden)],
                early_in.at[part],
                early_send.at[step],
                early_recv.at[part],
                device,
            ).start()

        loop(parts - 1, one)

    def grad_hidden_wait():
        def one(step, value):
            other, device = row_peer(step)
            remote(
                early_in.at[other],
                early_in.at[other],
                early_send.at[step],
                early_recv.at[other],
                device,
            ).wait()
            return value + early_in[other].astype(F32)

        return lax.fori_loop(
            0, parts - 1, one, early_out[:, lanes(part, hidden)].astype(F32)
        )

    def share_columns(whole, size, send_sem, recv_sem):
        def start(step):
            device = row_peer(step)[1]
            own = whole.at[:, lanes(part, size)]
            remote(own, own, send_sem.at[step], recv_sem.at[part], device).start()

        def wait(step):
            other, device = row_peer(step)
            theirs = whole.at[:, lanes(other, size)]
            remote(theirs, theirs, send_sem.at[step], recv_sem.at[other], device).wait()

        loop(parts - 1, start)
        loop(parts - 1, wait)

    def slopes(gate, up, grad_hidden):
        sigmoid = jax.nn.sigmoid(gate)
        grad_gate = grad_hidden * up * sigmoid * (1.0 + gate * (1.0 - sigmoid))
        grad_up = grad_hidden * gate * sigmoid
        return jnp.concatenate([grad_gate, grad_up], axis=1).astype(BF)

    def return_blocks(terms):
        up_one = (section, replica, away(1, 0))
        down_one = (section, replica, away(ring - 1, 0))
        plan = [
            (away(2, 0), up_one, 0),
            (away(2, 1), down_one, 1),
            (away(1, 1), None, None),
            (away(ring - 1, 1), None, None),
            (away(1, 0), None, None),
            (away(ring - 1, 0), None, None),
            (away(0, 1), None, None),
        ]
        sent = []
        for step, (block, device, way) in enumerate(plan):
            back_out[block] = dot_t(terms, gu[block]).astype(BF)
            target = back_in.at[part] if way is None else back_relay.at[way]
            arrived = back_recv.at[part] if way is None else back_relay_recv.at[way]
            copy = remote(
                back_out.at[block],
                target,
                back_send.at[step],
                arrived,
                (section, replica, block) if device is None else device,
            )
            copy.start()
            sent.append(copy)
        own = dot_t(terms, gu[part])
        for way in range(2):
            origin = away(ring - 1 - way * (ring - 2), 0)
            final = away(1 + way * (ring - 2), way)
            sent[way].wait_recv()
            copy = remote(
                back_relay.at[way],
                back_in.at[origin],
                back_relay_send.at[way],
                back_recv.at[origin],
                (section, replica, final),
            )
            copy.start()
            sent.append(copy)
        for block in (
            away(0, 1),
            away(1, 0),
            away(ring - 1, 0),
            away(1, 1),
            away(ring - 1, 1),
            away(2, 0),
            away(2, 1),
        ):
            remote(
                back_in.at[block],
                back_in.at[block],
                back_send.at[0],
                back_recv.at[block],
                (section, replica, block),
            ).wait_recv()
            own = own + back_in[block].astype(F32)
        for copy in sent:
            copy.wait_send()
        return own * gain

    over = remote(
        cross.at[0], cross.at[1], cross_send, cross_recv, (1 - section, replica, part)
    )

    @pl.when(section == 0)
    def _():
        rows = rows_ref[...].astype(F32)
        put_stats(0, [total(rows * rows)])
        share_stats(0)
        gate_up_start((rows * gain).astype(BF))
        wait_stats(0)
        scale = inverse(get_stats(0, 1)[0])
        whole = gate_up_wait() * scale
        hold[...] = whole
        gate = whole[:, :hidden]
        up = whole[:, hidden:]
        narrow_in[:, lanes(part, hidden)] = (gate * jax.nn.sigmoid(gate) * up).astype(BF)
        share_columns(narrow_in, hidden, narrow_send, narrow_recv)
        down_wait()
        out = rows_ref[...].astype(F32) + dot(narrow_in[...], down[...].reshape(parts * hidden, width))
        cross[0] = out.astype(BF)
        over.start()
        main = cross[0].astype(F32)
        put_stats(1, [total(main * main)])
        loop(parts, lambda step: tell_copy(step).start())
        loop(parts, lambda step: tell_copy(step).wait_send())
        over.wait()
        grad = cross[1]
        grad_hidden_start(grad)
        grad_hidden = grad_hidden_wait()
        whole = hold[...]
        wide_in[:, lanes(part, 2 * hidden)] = slopes(
            whole[:, :hidden], whole[:, hidden:], grad_hidden
        )
        put_stats(2, [total(wide_in[:, lanes(part, 2 * hidden)].astype(F32) * whole)])
        share_stats(2)
        share_columns(wide_in, 2 * hidden, wide_send, wide_recv)
        scaled = dot_t(wide_in[:, pl.ds(0, 2 * hidden)], gu[0])
        for index in range(1, parts):
            scaled = scaled + dot_t(
                wide_in[:, pl.ds(index * 2 * hidden, 2 * hidden)], gu[index]
            )
        scaled = scaled * gain
        rows = rows_ref[...].astype(F32)
        wait_stats(2)
        mean = get_stats(2, 1)[0] / model_width
        scale = inverse(get_stats(0, 1)[0])
        result = grad.astype(F32) + scale * scaled - rows * (scale * scale * mean)
        grad_ref[...] = result.astype(BF)

    @pl.when(section == 1)
    def _():
        rows = rows_ref[...].astype(F32)
        put_stats(0, [total(rows * rows)])
        share_stats(0)
        local_weights(lambda copy: copy.wait())
        cot_all[part] = mtp_cot_ref[...]
        grad_hidden = gather_dot(
            cot_all, cot_send, cot_recv, lambda block, index: dot_t(block, down[index])
        )
        wait_stats(0)
        scale_next = inverse(get_stats(0, 1)[0])

        def heard(index):
            remote(
                stat_in.at[1, index],
                stat_in.at[1, index],
                stat_send.at[1, 0],
                stat_recv.at[1, index],
                (1 - section, replica, part),
            ).wait_recv()

        loop(parts, heard)
        over.wait_recv()
        scale_main = inverse(get_stats(1, 1)[0])
        main = cross[1].astype(F32)
        mixed = (main * scale_main * gain_main + rows * scale_next * gain_next).astype(BF)
        mixed = mixed.astype(F32)
        put_stats(2, [total(mixed * mixed)])
        share_stats(2)
        mixed_all[part] = (mixed * gain).astype(BF)
        whole = gather_dot(
            mixed_all, mixed_send, mixed_recv, lambda block, index: dot(block, gu[index])
        )
        wait_stats(2)
        scale = inverse(get_stats(2, 1)[0])
        whole = whole * scale
        scaled = return_blocks(slopes(whole[:, :hidden], whole[:, hidden:], grad_hidden))
        cot = mtp_cot_ref[...].astype(F32)
        next_weighted = rows * gain_next
        main_weighted = main * gain_main
        put_stats(
            3,
            [
                total(mixed * scaled),
                total(next_weighted * scaled),
                total(next_weighted * mixed),
                total(next_weighted * cot),
                total(main_weighted * scaled),
                total(main_weighted * mixed),
                total(main_weighted * cot),
            ],
        )
        share_stats(3)
        wait_stats(3)
        s1, s2, s3, s4, s5, s6, s7 = get_stats(3, 7)
        slope = scale * scale * scale * (s1 / model_width)
        grad_mixed = cot + scale * scaled - mixed * slope
        mean_next = (s4 + scale * s2 - slope * s3) / model_width
        mean_main = (s7 + scale * s5 - slope * s6) / model_width
        grad_main = (
            main_cot_ref[...].astype(F32)
            + scale_main * (gain_main * grad_mixed)
            - main * (scale_main * scale_main * scale_main * mean_main)
        )
        cross[0] = grad_main.astype(BF)
        over.start()
        grad_next = scale_next * (gain_next * grad_mixed) - rows * (
            scale_next * scale_next * scale_next * mean_next
        )
        grad_ref[...] = grad_next.astype(BF)
        over.wait_send()

    loop(replicas - 1, lambda step: row_copy(step).wait_send())
    slot_back = to_row(slot_column).astype(jnp.int32)
    group_rows = group * half

    def pack_rows(side, put):
        def pack(block):
            base = (side * (replicas // group) + block) * group_rows
            hit = slot_back == iota((group_rows, tokens), 0) + base
            found = dot(jnp.where(hit, 1.0, 0.0).astype(BF), grad_ref[...]).astype(BF)
            put(pl.ds(block * group, group), found.reshape(group, half, width))

        if group == replicas:
            pack(0)
        else:
            loop(replicas // group, pack)

    def sum_copy(step):
        other, device = column_peer(step)
        return remote(
            send.at[other],
            sums_ref.at[section, replica],
            sum_send.at[step],
            sum_recv.at[replica],
            device,
        )

    pack_rows(1 - section, put_swap)
    swap_copy(1).start()
    pack_rows(section, put_send)
    swap_copy(1).wait()
    send[...] = send[...] + swap_in[...]
    loop(replicas - 1, lambda step: sum_copy(step).start())
    sums_ref[section, replica] = send[replica]

    @pl.when(section == 0)
    def _():
        for kind in range(3):
            for way in range(2):
                relay_copy(kind, way).wait_send()
                forward_copy(kind, way).wait_send()
            loop(parts - 3, lambda step: direct_copy(kind, step).wait_send())

    collect(sums_ref, 1, sum_send, sum_recv)
    loop(replicas - 1, lambda step: sum_copy(step).wait_send())


def place_kernel(lid_ref, sums_ref, out_ref):
    rows = out_ref.shape[0]
    slots = sums_ref.shape[0]
    base = pl.program_id(0) * rows
    hit = lid_ref[0:1, :] == iota((rows, slots), 0) + base
    out_ref[...] = dot(jnp.where(hit, 1.0, 0.0).astype(BF), sums_ref[...]).astype(BF)


def vmem():
    return pl.BlockSpec(memory_space=pltpu.VMEM)


def anywhere():
    return pl.BlockSpec(memory_space=pl.ANY)


def dma(*shape):
    return pltpu.SemaphoreType.DMA(shape)


def train_step(
    per_pair,
    token_ids,
    next_ids,
    embed_table,
    norm_gain,
    w_gate,
    w_up,
    w_down,
    mtp_gain,
    main_cot,
    mtp_cot,
):
    sections = lax.axis_size("section")
    replicas = lax.axis_size("dp")
    parts = lax.axis_size("mp")
    count = sections * replicas
    batches = token_ids.shape[0]
    tokens = batches * (token_ids.shape[1] // replicas)
    vocab_rows, width = embed_table.shape
    hidden = w_gate.shape[2]
    half = per_pair // 2
    slots = replicas * per_pair
    picked = min(replicas * half, max(2 * tokens, half))
    block = pltpu.VMEM((parts, tokens, width), BF)
    one = pltpu.SemaphoreType.DMA
    return pl.pallas_call(
        functools.partial(step_kernel, sections, replicas, parts, per_pair),
        out_shape=(
            jax.ShapeDtypeStruct((2, replicas, half, width), BF),
            jax.ShapeDtypeStruct((8, slots), jnp.int32),
            jax.ShapeDtypeStruct((8, 128), F32),
        ),
        in_specs=[vmem()] * 6 + [anywhere()] * 4,
        out_specs=(vmem(), vmem(), vmem()),
        scratch_shapes=[
            pltpu.VMEM((vocab_rows, width), BF),
            pltpu.VMEM((count, tokens), F32),
            pltpu.VMEM((count, tokens), F32),
            pltpu.VMEM((count, tokens), F32),
            pltpu.VMEM((slots, tokens), jnp.int32),
            pltpu.VMEM((picked, vocab_rows), BF),
            pltpu.VMEM((replicas, half, width), BF),
            pltpu.VMEM((replicas, half, width), BF),
            pltpu.VMEM((replicas, half, width), BF),
            pltpu.VMEM((2, replicas, half, width), BF),
            pltpu.VMEM((tokens, width), BF),
            pltpu.VMEM((tokens, width), BF),
            pltpu.VMEM((parts, width, 2 * hidden), BF),
            pltpu.VMEM((parts, hidden, width), BF),
            pltpu.VMEM((2, width, 2 * hidden), BF),
            pltpu.VMEM((2, hidden, width), BF),
            pltpu.VMEM((parts, tokens, 2 * hidden), BF),
            pltpu.VMEM((parts, tokens, 2 * hidden), BF),
            pltpu.VMEM((tokens, parts * hidden), BF),
            pltpu.VMEM((parts, tokens, hidden), BF),
            pltpu.VMEM((tokens, parts * hidden), BF),
            pltpu.VMEM((tokens, parts * 2 * hidden), BF),
            pltpu.VMEM((4, parts, 8, tokens), F32),
            block,
            block,
            block,
            block,
            pltpu.VMEM((2, tokens, width), BF),
            pltpu.VMEM((2, tokens, width), BF),
            pltpu.VMEM((tokens, 2 * hidden), F32),
            one,
            one,
            dma(2),
            dma(2),
            dma(replicas),
            dma(replicas),
            dma(replicas),
            dma(replicas),
            dma(2, replicas),
            dma(2, replicas),
            dma(3),
            dma(3, parts),
            dma(3, parts),
            dma(3, parts),
            dma(3, 2),
            dma(3, 2),
        ]
        + [dma(parts)] * 8
        + [dma(4, parts)] * 2
        + [one] * 2
        + [dma(parts)] * 6
        + [dma(2)] * 2,
        compiler_params=pltpu.CompilerParams(
            collective_id=0 if per_pair == FEW_SLOTS else 1,
            has_side_effects=True,
            vmem_limit_bytes=60 << 20,
        ),
        name=f"train_step_{per_pair}",
    )(
        token_ids,
        next_ids,
        main_cot.reshape(tokens, width),
        mtp_cot.reshape(tokens, width),
        norm_gain,
        mtp_gain,
        embed_table,
        w_gate[0],
        w_up[0],
        w_down[0],
    )


def place(lid_row, sums, vocab_rows):
    width = sums.shape[-1]
    slots = lid_row.shape[1]
    block = vocab_rows // 8
    return pl.pallas_call(
        place_kernel,
        grid=(vocab_rows // block,),
        out_shape=jax.ShapeDtypeStruct((vocab_rows, width), BF),
        in_specs=[
            pl.BlockSpec((8, slots), lambda i: (0, 0)),
            pl.BlockSpec((slots, width), lambda i: (0, 0)),
        ],
        out_specs=pl.BlockSpec((block, width), lambda i: (i, 0)),
        compiler_params=pltpu.CompilerParams(vmem_limit_bytes=56 << 20),
        name="place_rows",
    )(lid_row, sums.reshape(slots, width))


def body(*arguments):
    vocab_rows = arguments[2].shape[0]
    positions = 2 * arguments[0].shape[0] * (arguments[0].shape[1] // lax.axis_size("dp"))
    sums, lid_row, most = train_step(FEW_SLOTS, *arguments)

    def few(sums, lid_row, *given):
        return place(lid_row, sums, vocab_rows)

    def many(sums, lid_row, *given):
        sums, lid_row, most = train_step(positions, *given)
        return place(lid_row, sums, vocab_rows)

    return lax.cond(most[0, 0] <= FEW_SLOTS, few, many, sums, lid_row, *arguments)


def solution(mesh):
    return jax.shard_map(
        body,
        mesh=mesh,
        in_specs=(
            P(),
            P(),
            P(("section", "dp"), "mp"),
            P("section", None),
            P("section", None, "mp"),
            P("section", None, "mp"),
            P("section", "mp", None),
            P(),
            P(None, "dp", "mp"),
            P(None, "dp", "mp"),
        ),
        out_specs=P(("section", "dp"), "mp"),
        check_vma=False,
    )
```

```python
import functools

import jax
import jax.numpy as jnp
from jax import lax
from jax.experimental import pallas as pl
from jax.experimental.pallas import tpu as pltpu
from jax.sharding import PartitionSpec as P

EPS = 1e-06
MESH = pl.DeviceIdType.MESH
FEW_SLOTS = 32
BF = jnp.bfloat16
F32 = jnp.float32
COLS = (((1,), (1,)), ((), ()))


def dot(a, b):
    return jnp.dot(a, b, preferred_element_type=F32)


def dot_t(a, b):
    return lax.dot_general(a, b, COLS, preferred_element_type=F32)


def iota(shape, axis):
    return lax.broadcasted_iota(jnp.int32, shape, axis)


def loop(count, one):
    def step(index, carry):
        one(index)
        return carry

    lax.fori_loop(0, count, step, 0)


def remote(source, target, send_sem, recv_sem, device):
    return pltpu.make_async_remote_copy(
        src_ref=source,
        dst_ref=target,
        send_sem=send_sem,
        recv_sem=recv_sem,
        device_id=device,
        device_id_type=MESH,
    )


def to_column(row):
    count = row.shape[1]
    eye = iota((count, count), 0) == iota((count, count), 1)
    whole = jnp.broadcast_to(row, (count, count))
    return jnp.sum(jnp.where(eye, whole, jnp.zeros_like(whole)), axis=1, keepdims=True)


def to_row(column):
    count = column.shape[0]
    eye = iota((count, count), 0) == iota((count, count), 1)
    whole = jnp.broadcast_to(column, (count, count))
    return jnp.sum(jnp.where(eye, whole, jnp.zeros_like(whole)), axis=0, keepdims=True)


def total(values):
    return jnp.sum(values, axis=1, keepdims=True)


def step_kernel(
    sections,
    replicas,
    parts,
    per_pair,
    token_ids_ref,
    next_ids_ref,
    main_cot_ref,
    mtp_cot_ref,
    gain_ref,
    mtp_gain_ref,
    table_hbm,
    gate_hbm,
    up_hbm,
    down_hbm,
    sums_ref,
    lid_ref,
    over_ref,
    table,
    ids_ref,
    first,
    rank,
    lid,
    onehot,
    send,
    swap_out,
    swap_in,
    recv,
    rows_ref,
    grad_ref,
    gu,
    down,
    relay_gu,
    relay_down,
    part_out,
    part_in,
    early_out,
    early_in,
    narrow_in,
    wide_in,
    stat_in,
    mixed_all,
    cot_all,
    back_out,
    back_in,
    back_relay,
    cross,
    hold,
    table_sem,
    local_sem,
    swap_send,
    swap_recv,
    row_send,
    row_recv,
    sum_send,
    sum_recv,
    pass_send,
    pass_recv,
    weight_local,
    local_weight,
    weight_send,
    weight_recv,
    relay_send,
    relay_recv,
    across_send,
    part_send,
    part_recv,
    early_send,
    early_recv,
    wide_send,
    wide_recv,
    narrow_send,
    narrow_recv,
    stat_send,
    stat_recv,
    cross_send,
    cross_recv,
    mixed_send,
    mixed_recv,
    cot_send,
    cot_recv,
    back_send,
    back_recv,
    back_relay_recv,
):
    section = lax.axis_index("section")
    replica = lax.axis_index("dp")
    part = lax.axis_index("mp")
    count = sections * replicas
    me = section * replicas + replica
    vocab_rows, width = table_hbm.shape
    hidden = gate_hbm.shape[1]
    batches = token_ids_ref.shape[0]
    tokens = ids_ref.shape[1]
    run = tokens // batches
    model_width = parts * width
    half = per_pair // 2
    slots = replicas * per_pair
    ring = parts // 2
    load = pltpu.make_async_copy(table_hbm, table, table_sem)
    load.start()

    def column_peer(step):
        other = lax.rem(replica + 1 + step, replicas)
        return other, (section, other, part)

    partner = (1 - section, replica, part)

    def away(ahead, across):
        return lax.rem(part // 2 + ahead, ring) * 2 + lax.rem(part + across, 2)

    def row_peer(step):
        ahead = jnp.where(
            step < 2,
            1 + step * (ring - 2),
            jnp.where(step == 2, 0, jnp.where(step < 5, 1 + (step - 3) * (ring - 2), 2)),
        )
        across = jnp.where(step < 2, 0, jnp.where(step < 5, 1, step - 5))
        other = away(ahead, across)
        return other, (section, replica, other)

    barrier = pltpu.get_barrier_semaphore()

    def greet_column(step):
        device = column_peer(step)[1]
        pl.semaphore_signal(barrier, inc=1, device_id=device, device_id_type=MESH)

    def greet_row(step):
        other = lax.rem(part + 1 + lax.rem(step, parts), parts)
        there = jnp.where(step < parts - 1, section, 1 - section)
        other = jnp.where(step < parts - 1, other, lax.rem(part + step, parts))
        pl.semaphore_signal(
            barrier, inc=1, device_id=(there, replica, other), device_id_type=MESH
        )

    loop(replicas - 1, greet_column)
    loop(2 * parts - 1, greet_row)

    rows_of = 2 * batches
    row_index = lax.rem(iota((rows_of, tokens), 0), batches)
    own_run = iota((rows_of, tokens), 1) // run == row_index
    for group in range(replicas // batches):
        columns = pl.ds(group * tokens, tokens)
        both = jnp.concatenate(
            [token_ids_ref[:, columns], next_ids_ref[:, columns]], axis=0
        ).astype(F32)
        turned = [both] + [pltpu.roll(both, shift * run, 1) for shift in range(1, batches)]
        for inner in range(batches):
            value = jnp.zeros_like(both)
            for shift in range(batches):
                wanted = own_run & (lax.rem(row_index - inner + batches, batches) == shift)
                value = jnp.where(wanted, turned[shift], value)
            index = group * batches + inner
            ids_ref[index : index + 1, :] = jnp.sum(value[:batches], axis=0, keepdims=True)
            ids_ref[replicas + index : replicas + index + 1, :] = jnp.sum(
                value[batches:], axis=0, keepdims=True
            )

    earlier = iota((tokens, tokens), 0) < iota((tokens, tokens), 1)

    def find_first(step):
        for inner in range(4):
            index = pl.ds(step * 4 + inner, 1)
            row = ids_ref[index, :]
            same = (to_column(row) == row) & earlier
            seen = jnp.max(jnp.where(same, 1.0, 0.0), axis=0, keepdims=True)
            first[index, :] = 1.0 - seen

    loop(count // 4, find_first)
    pl.semaphore_wait(barrier, replicas - 1 + 2 * parts - 1)

    def weight_source(target):
        features = pl.ds(pl.multiple_of(target * width, width), width)
        return gate_hbm.at[features, :], up_hbm.at[features, :], down_hbm.at[:, features]

    def weight_slot(origin):
        return (
            gu.at[origin, :, pl.ds(0, hidden)],
            gu.at[origin, :, pl.ds(hidden, hidden)],
            down.at[origin],
        )

    def relay_slot(way):
        return (
            relay_gu.at[way, :, pl.ds(0, hidden)],
            relay_gu.at[way, :, pl.ds(hidden, hidden)],
            relay_down.at[way],
        )

    def direct_copy(kind, step):
        other, device = row_peer(step)
        return remote(
            weight_source(other)[kind],
            weight_slot(part)[kind],
            weight_send.at[kind, step],
            weight_recv.at[kind, part],
            device,
        )

    def relay_copy(kind, way):
        final = away(2, way)
        return remote(
            weight_source(final)[kind],
            relay_slot(way)[kind],
            weight_send.at[kind, parts - 3 + way],
            relay_recv.at[kind, way],
            (section, replica, away(1 + way * (ring - 2), 0)),
        )

    def forward_copy(kind, way):
        origin = away(ring - 1 - way * (ring - 2), 0)
        final = away(1 + way * (ring - 2), way)
        return remote(
            relay_slot(way)[kind],
            weight_slot(origin)[kind],
            relay_send.at[kind, way],
            weight_recv.at[kind, origin],
            (section, replica, final),
        )

    def own_weight(kind):
        return pltpu.make_async_copy(
            weight_source(part)[kind], weight_slot(part)[kind], weight_local.at[kind]
        )

    def local_weights(then):
        def one(target):
            for kind, source in enumerate(weight_source(target)):
                then(
                    pltpu.make_async_copy(
                        source, weight_slot(target)[kind], local_weight.at[kind, target]
                    )
                )

        loop(parts, one)

    level = lax.rem(replica // 2, 2)
    across = (section, replica + 2 - 4 * level, part)

    def by_level(then, swap=0):
        for value in range(2):

            @pl.when(level == value)
            def _():
                then(value if swap == 0 else 1 - value)

    def weights_begin(kind):
        for way in range(2):
            relay_copy(kind, way).start()
        loop(parts - 3, lambda step: direct_copy(kind, step).start())

    def weights_start():
        by_level(weights_begin)
        weights_begin(2)
        for kind in range(3):
            own_weight(kind).start()

    def relay_on(kinds):
        for kind in kinds:
            for way in range(2):
                relay_copy(kind, way).wait_recv()
                forward_copy(kind, way).start()

    def weight_wait(kind, step):
        other, device = row_peer(step)
        remote(
            weight_slot(other)[kind],
            weight_slot(other)[kind],
            weight_send.at[kind, step],
            weight_recv.at[kind, other],
            device,
        ).wait_recv()

    def across_copy(kind, step):
        other = row_peer(step)[0]
        slot = weight_slot(other)[kind]
        return remote(
            slot, slot, across_send.at[step], weight_recv.at[kind, other], across
        )

    def hand_across(kind):
        def one(step):
            weight_wait(kind, step)
            across_copy(kind, step).start()

        loop(parts - 1, one)

    def weights_done(kind):
        for way in range(2):
            relay_copy(kind, way).wait_send()
            forward_copy(kind, way).wait_send()
        loop(parts - 3, lambda step: direct_copy(kind, step).wait_send())

    def across_done(kind):
        loop(parts - 1, lambda step: across_copy(kind, step).wait_send())

    @pl.when(section == 0)
    def _():
        weights_start()

    @pl.when(section == 1)
    def _():
        local_weights(lambda copy: copy.start())

    def shard_of(rows):
        return jnp.floor(rows * (1.0 / vocab_rows))

    def chip_of(rows):
        shards = shard_of(rows)
        return shards - replicas * jnp.floor(shards * (1.0 / replicas))

    triangle = jnp.where(earlier, 1.0, 0.0).astype(BF)
    me_f = me.astype(F32)
    here_f = replica.astype(F32)
    group = min(replicas, max(1, 2 * tokens // half))

    def row_copy(step):
        other, device = column_peer(step)
        return remote(
            send.at[other],
            recv.at[section, replica],
            row_send.at[step],
            row_recv.at[replica],
            device,
        )

    def ranks(first_row):
        rows = pl.ds(first_row, replicas)
        mine = jnp.where(chip_of(ids_ref[rows, :]) == here_f, first[rows, :], 0.0)
        return mine, dot(mine.astype(BF), triangle)

    mine, order = ranks(0)
    before = total(mine)
    rank[pl.ds(0, replicas), :] = jnp.where(mine > 0.0, order, -1.0)
    mine, order = ranks(replicas)
    rank[pl.ds(replicas, replicas), :] = jnp.where(mine > 0.0, order + before, -1.0)

    def find_lid(step):
        for inner in range(2):
            index = step * 2 + inner
            found = jnp.zeros((per_pair, 1), F32)
            for offset in (0, replicas):
                row = ids_ref[pl.ds(index + offset, 1), :] - (me_f * vocab_rows - 1.0)
                picks = rank[pl.ds(index + offset, 1), :].astype(jnp.int32) == iota(
                    (per_pair, tokens), 0
                )
                found += total(jnp.where(picks, jnp.broadcast_to(row, picks.shape), 0.0))
            whole = jnp.broadcast_to(found - 1.0, (per_pair, tokens)).astype(jnp.int32)
            for side in range(2):
                place = pl.multiple_of((side * replicas + index) * half, half)
                lid[pl.ds(place, half), :] = whole[side * half : (side + 1) * half]

    loop(replicas // 2, find_lid)

    def pick_rows(side, put):
        def chunk(block):
            base = block * group

            def mark(step):
                place = pl.multiple_of((side * replicas + base + step) * half, half)
                wanted = lid[pl.ds(place, half), :]
                there = pl.ds(pl.multiple_of(step * half, half), half)
                for lane in range(vocab_rows // tokens):
                    hit = wanted == iota(wanted.shape, 1) + lane * tokens
                    onehot[there, pl.ds(lane * tokens, tokens)] = jnp.where(
                        hit, 1.0, 0.0
                    ).astype(BF)

            loop(group, mark)
            found = dot(onehot[...], table[...]).astype(BF)
            put(pl.ds(base, group), found.reshape(group, half, width))

        if group == replicas:
            chunk(0)
        else:
            loop(replicas // group, chunk)

    def swap_copy(turn):
        return remote(
            swap_out, swap_in, swap_send.at[turn], swap_recv.at[turn], partner
        )

    def put_swap(place, values):
        swap_out[place] = values

    def put_send(place, values):
        send[place] = values

    load.wait()
    pick_rows(1 - section, put_swap)
    swap_copy(0).start()
    pick_rows(section, put_send)
    swap_copy(0).wait()
    send[...] = send[...] + swap_in[...]
    loop(replicas - 1, lambda step: row_copy(step).start())
    recv[section, replica] = send[replica]

    @pl.when(section == 0)
    def _():
        by_level(lambda kind: relay_on((kind,)))
        by_level(hand_across)
        relay_on((2,))

    chip = chip_of(ids_ref[...])

    def fill(step, most):
        for inner in range(4):
            held = jnp.where(chip == (step * 4 + inner).astype(F32), first[...], 0.0)
            held = total(held)
            most = jnp.maximum(most, held[:replicas] + held[replicas:])
        return most

    most = lax.fori_loop(0, replicas // 4, fill, jnp.zeros((replicas, 1), F32))
    over_ref[...] = jnp.broadcast_to(jnp.max(most, axis=0, keepdims=True), over_ref.shape)
    eye = iota((tokens, tokens), 0) == iota((tokens, tokens), 1)

    def turn(block):
        rows = pl.ds(pl.multiple_of(block * tokens, tokens), tokens)
        row = jnp.sum(jnp.where(eye, lid[rows, :], 0), axis=0, keepdims=True)
        lid_ref[:, rows] = jnp.broadcast_to(row, (8, tokens))

    loop(slots // tokens, turn)
    own_row = ids_ref[pl.ds(me, 1), :]
    own_first = first[pl.ds(me, 1), :]
    own_column = to_column(own_row)
    chip_row = chip_of(own_row)
    counted = (chip_of(own_column) == chip_row) & earlier & (to_column(own_first) > 0.0)
    main_chip = chip_of(to_column(ids_ref[pl.ds(replica, 1), :]))
    main_first = to_column(first[pl.ds(replica, 1), :])
    ahead = jnp.where((main_chip == chip_row) & (main_first > 0.0), 1.0, 0.0)
    rank_row = jnp.sum(
        jnp.where(counted, 1.0, 0.0) + ahead * section.astype(F32), axis=0, keepdims=True
    )
    side_row = jnp.floor(rank_row * (1.0 / half))
    slot_row = (side_row * (replicas - 1) + chip_row) * half + rank_row
    leads = (own_column == own_row) & (own_first > 0.0)
    slot_column = total(jnp.where(leads, jnp.broadcast_to(slot_row, leads.shape), 0.0))

    def pass_copy(whole, turn, block):
        return remote(
            whole.at[section, block],
            whole.at[section, block],
            pass_send.at[turn, block],
            pass_recv.at[turn, block],
            partner,
        )

    def collect(whole, turn, send_sem, recv_sem):
        pass_copy(whole, turn, replica).start()

        def arrive(step):
            other = lax.rem(replica + replicas - 1 - step, replicas)
            remote(
                whole.at[section, other],
                whole.at[section, other],
                send_sem.at[step],
                recv_sem.at[other],
                partner,
            ).wait_recv()
            pass_copy(whole, turn, other).start()

        def passed(block):
            remote(
                whole.at[1 - section, block],
                whole.at[1 - section, block],
                pass_send.at[turn, block],
                pass_recv.at[turn, block],
                partner,
            ).wait()

        loop(replicas - 1, arrive)
        loop(replicas, passed)

    def block_copy(whole, send_sem, recv_sem, block, step, device):
        return remote(
            whole.at[block], whole.at[block], send_sem.at[step], recv_sem.at[block], device
        )

    def gather_blocks(whole, send_sem, recv_sem, use):
        up_one = (section, replica, away(1, 0))
        down_one = (section, replica, away(ring - 1, 0))
        beside = (section, replica, away(0, 1))
        plan = [
            (away(0, 0), (up_one, down_one, beside)),
            (away(0, 1), (up_one, down_one)),
            (away(ring - 1, 0), (up_one,)),
            (away(1, 0), ()),
            (away(1, 1), (down_one,)),
            (away(ring - 1, 1), ()),
            (away(2, 0), ()),
            (away(2, 1), ()),
        ]
        step = 0
        sent = []
        for position, (block, devices) in enumerate(plan):
            if position > 0:
                block_copy(whole, send_sem, recv_sem, block, 0, beside).wait_recv()
            for device in devices:
                copy = block_copy(whole, send_sem, recv_sem, block, step, device)
                copy.start()
                sent.append(copy)
                step += 1
            use(block)
        for copy in sent:
            copy.wait_send()

    def gather_dot(whole, send_sem, recv_sem, product):
        held = []

        def use(block):
            held.append(product(whole[block], block))

        gather_blocks(whole, send_sem, recv_sem, use)
        value = held[0]
        for other in held[1:]:
            value = value + other
        return value

    collect(recv, 0, row_send, row_recv)
    slot_of = slot_column.astype(jnp.int32)
    spread = jnp.where(slot_of == iota((tokens, slots), 1), 1.0, 0.0).astype(BF)
    rows_ref[...] = dot(spread, recv[...].reshape(slots, width)).astype(BF)

    features = pl.ds(pl.multiple_of(part * width, width), width)
    gain = gain_ref[0:1, features]
    gain_main = mtp_gain_ref[0:1, features]
    gain_next = mtp_gain_ref[1:2, features]

    def inverse(sum_of_squares):
        return lax.rsqrt(sum_of_squares / model_width + EPS)

    def lanes(index, size):
        return pl.ds(pl.multiple_of(index * size, size), size)

    def put_stats(slot, columns):
        rows = [to_row(column) for column in columns]
        rows = rows + [jnp.zeros_like(rows[0])] * (8 - len(rows))
        stat_in[slot, part] = jnp.concatenate(rows, axis=0)

    def get_stats(slot, number):
        value = stat_in[slot, 0]
        for index in range(1, parts):
            value = value + stat_in[slot, index]
        return [to_column(value[index : index + 1, :]) for index in range(number)]

    def stat_copy(slot, step):
        return remote(
            stat_in.at[slot, part],
            stat_in.at[slot, part],
            stat_send.at[slot, step],
            stat_recv.at[slot, part],
            row_peer(step)[1],
        )

    def share_stats(slot):
        loop(parts - 1, lambda step: stat_copy(slot, step).start())

    def wait_stats(slot):
        def one(step):
            other, device = row_peer(step)
            remote(
                stat_in.at[slot, other],
                stat_in.at[slot, other],
                stat_send.at[slot, step],
                stat_recv.at[slot, other],
                device,
            ).wait()

        loop(parts - 1, one)

    def tell_copy(step):
        other = lax.rem(part + step, parts)
        return remote(
            stat_in.at[1, part],
            stat_in.at[1, part],
            stat_send.at[1, step],
            stat_recv.at[1, part],
            (1 - section, replica, other),
        )

    def gate_up_start(normed):
        def partial(other):
            part_out[other] = dot(normed, gu[other]).astype(BF)

        def one(step):
            other, device = row_peer(step)
            by_level(lambda kind: weight_wait(kind, step), swap=1)
            partial(other)
            remote(
                part_out.at[other],
                part_in.at[part],
                part_send.at[step],
                part_recv.at[part],
                device,
            ).start()

        loop(parts - 1, one)
        own_weight(0).wait()
        own_weight(1).wait()
        partial(part)

    def gate_up_wait():
        def one(step, value):
            other, device = row_peer(step)
            remote(
                part_in.at[other],
                part_in.at[other],
                part_send.at[step],
                part_recv.at[other],
                device,
            ).wait()
            return value + part_in[other].astype(F32)

        return lax.fori_loop(0, parts - 1, one, part_out[part].astype(F32))

    def down_wait():
        loop(parts - 1, lambda step: weight_wait(2, step))
        own_weight(2).wait()

    def grad_hidden_start(grad):
        early_out[...] = dot_t(grad, down[...].reshape(parts * hidden, width)).astype(BF)

        def one(step):
            other, device = row_peer(step)
            remote(
                early_out.at[:, lanes(other, hidden)],
                early_in.at[part],
                early_send.at[step],
                early_recv.at[part],
                device,
            ).start()

        loop(parts - 1, one)

    def grad_hidden_wait():
        def one(step, value):
            other, device = row_peer(step)
            remote(
                early_in.at[other],
                early_in.at[other],
                early_send.at[step],
                early_recv.at[other],
                device,
            ).wait()
            return value + early_in[other].astype(F32)

        return lax.fori_loop(
            0, parts - 1, one, early_out[:, lanes(part, hidden)].astype(F32)
        )

    def share_columns(whole, size, send_sem, recv_sem):
        def start(step):
            device = row_peer(step)[1]
            own = whole.at[:, lanes(part, size)]
            remote(own, own, send_sem.at[step], recv_sem.at[part], device).start()

        def wait(step):
            other, device = row_peer(step)
            theirs = whole.at[:, lanes(other, size)]
            remote(theirs, theirs, send_sem.at[step], recv_sem.at[other], device).wait()

        loop(parts - 1, start)
        loop(parts - 1, wait)

    def slopes(gate, up, grad_hidden):
        sigmoid = jax.nn.sigmoid(gate)
        grad_gate = grad_hidden * up * sigmoid * (1.0 + gate * (1.0 - sigmoid))
        grad_up = grad_hidden * gate * sigmoid
        return jnp.concatenate([grad_gate, grad_up], axis=1).astype(BF)

    def return_blocks(terms):
        up_one = (section, replica, away(1, 0))
        down_one = (section, replica, away(ring - 1, 0))
        sent = []

        def go(block, values, target, arrived, device):
            back_out[block] = values.astype(BF)
            copy = remote(
                back_out.at[block], target, back_send.at[len(sent)], arrived, device
            )
            copy.start()
            sent.append(copy)

        for way, device in enumerate((up_one, down_one)):
            block = away(2, way)
            values = dot_t(terms, gu[block])
            go(block, values, back_relay.at[way], back_relay_recv.at[way], device)
        for block in (away(1, 1), away(ring - 1, 0), away(0, 1)):
            values = dot_t(terms, gu[block])
            device = (section, replica, block)
            go(block, values, back_in.at[part], back_recv.at[part], device)
        for way, block in enumerate((away(1, 0), away(ring - 1, 1))):
            values = dot_t(terms, gu[block])
            sent[way].wait_recv()
            device = (section, replica, block)
            values = values + back_relay[way].astype(F32)
            go(block, values, back_in.at[part], back_recv.at[part], device)
        own = dot_t(terms, gu[part])
        for block in (
            away(0, 1),
            away(1, 0),
            away(ring - 1, 1),
            away(ring - 1, 0),
            away(1, 1),
        ):
            remote(
                back_in.at[block],
                back_in.at[block],
                back_send.at[0],
                back_recv.at[block],
                (section, replica, block),
            ).wait_recv()
            own = own + back_in[block].astype(F32)
        for copy in sent:
            copy.wait_send()
        return own * gain

    over = remote(
        cross.at[0], cross.at[1], cross_send, cross_recv, (1 - section, replica, part)
    )

    @pl.when(section == 0)
    def _():
        rows = rows_ref[...].astype(F32)
        put_stats(0, [total(rows * rows)])
        share_stats(0)
        gate_up_start((rows * gain).astype(BF))
        wait_stats(0)
        scale = inverse(get_stats(0, 1)[0])
        whole = gate_up_wait() * scale
        hold[...] = whole
        gate = whole[:, :hidden]
        up = whole[:, hidden:]
        narrow_in[:, lanes(part, hidden)] = (gate * jax.nn.sigmoid(gate) * up).astype(BF)
        share_columns(narrow_in, hidden, narrow_send, narrow_recv)
        down_wait()
        out = rows_ref[...].astype(F32) + dot(narrow_in[...], down[...].reshape(parts * hidden, width))
        cross[0] = out.astype(BF)
        over.start()
        main = cross[0].astype(F32)
        put_stats(1, [total(main * main)])
        loop(parts, lambda step: tell_copy(step).start())
        loop(parts, lambda step: tell_copy(step).wait_send())
        over.wait()
        grad = cross[1]
        grad_hidden_start(grad)
        grad_hidden = grad_hidden_wait()
        whole = hold[...]
        wide_in[:, lanes(part, 2 * hidden)] = slopes(
            whole[:, :hidden], whole[:, hidden:], grad_hidden
        )
        put_stats(2, [total(wide_in[:, lanes(part, 2 * hidden)].astype(F32) * whole)])
        share_stats(2)
        share_columns(wide_in, 2 * hidden, wide_send, wide_recv)
        scaled = dot_t(wide_in[:, pl.ds(0, 2 * hidden)], gu[0])
        for index in range(1, parts):
            scaled = scaled + dot_t(
                wide_in[:, pl.ds(index * 2 * hidden, 2 * hidden)], gu[index]
            )
        scaled = scaled * gain
        rows = rows_ref[...].astype(F32)
        wait_stats(2)
        mean = get_stats(2, 1)[0] / model_width
        scale = inverse(get_stats(0, 1)[0])
        result = grad.astype(F32) + scale * scaled - rows * (scale * scale * mean)
        grad_ref[...] = result.astype(BF)

    @pl.when(section == 1)
    def _():
        rows = rows_ref[...].astype(F32)
        put_stats(0, [total(rows * rows)])
        share_stats(0)
        local_weights(lambda copy: copy.wait())
        cot_all[part] = mtp_cot_ref[...]
        grad_hidden = gather_dot(
            cot_all, cot_send, cot_recv, lambda block, index: dot_t(block, down[index])
        )
        wait_stats(0)
        scale_next = inverse(get_stats(0, 1)[0])

        def heard(index):
            remote(
                stat_in.at[1, index],
                stat_in.at[1, index],
                stat_send.at[1, 0],
                stat_recv.at[1, index],
                (1 - section, replica, part),
            ).wait_recv()

        loop(parts, heard)
        over.wait_recv()
        scale_main = inverse(get_stats(1, 1)[0])
        main = cross[1].astype(F32)
        mixed = (main * scale_main * gain_main + rows * scale_next * gain_next).astype(BF)
        mixed = mixed.astype(F32)
        put_stats(2, [total(mixed * mixed)])
        share_stats(2)
        mixed_all[part] = (mixed * gain).astype(BF)
        whole = gather_dot(
            mixed_all, mixed_send, mixed_recv, lambda block, index: dot(block, gu[index])
        )
        wait_stats(2)
        scale = inverse(get_stats(2, 1)[0])
        whole = whole * scale
        scaled = return_blocks(slopes(whole[:, :hidden], whole[:, hidden:], grad_hidden))
        cot = mtp_cot_ref[...].astype(F32)
        next_weighted = rows * gain_next
        main_weighted = main * gain_main
        put_stats(
            3,
            [
                total(mixed * scaled),
                total(next_weighted * scaled),
                total(next_weighted * mixed),
                total(next_weighted * cot),
                total(main_weighted * scaled),
                total(main_weighted * mixed),
                total(main_weighted * cot),
            ],
        )
        share_stats(3)
        wait_stats(3)
        s1, s2, s3, s4, s5, s6, s7 = get_stats(3, 7)
        slope = scale * scale * scale * (s1 / model_width)
        grad_mixed = cot + scale * scaled - mixed * slope
        mean_next = (s4 + scale * s2 - slope * s3) / model_width
        mean_main = (s7 + scale * s5 - slope * s6) / model_width
        grad_main = (
            main_cot_ref[...].astype(F32)
            + scale_main * (gain_main * grad_mixed)
            - main * (scale_main * scale_main * scale_main * mean_main)
        )
        cross[0] = grad_main.astype(BF)
        over.start()
        grad_next = scale_next * (gain_next * grad_mixed) - rows * (
            scale_next * scale_next * scale_next * mean_next
        )
        grad_ref[...] = grad_next.astype(BF)
        over.wait_send()

    loop(replicas - 1, lambda step: row_copy(step).wait_send())
    slot_back = to_row(slot_column).astype(jnp.int32)
    group_rows = group * half

    def pack_rows(side, put):
        def pack(block):
            base = (side * (replicas // group) + block) * group_rows
            hit = slot_back == iota((group_rows, tokens), 0) + base
            found = dot(jnp.where(hit, 1.0, 0.0).astype(BF), grad_ref[...]).astype(BF)
            put(pl.ds(block * group, group), found.reshape(group, half, width))

        if group == replicas:
            pack(0)
        else:
            loop(replicas // group, pack)

    def sum_copy(step):
        other, device = column_peer(step)
        return remote(
            send.at[other],
            sums_ref.at[section, replica],
            sum_send.at[step],
            sum_recv.at[replica],
            device,
        )

    pack_rows(1 - section, put_swap)
    swap_copy(1).start()
    pack_rows(section, put_send)
    swap_copy(1).wait()
    send[...] = send[...] + swap_in[...]
    loop(replicas - 1, lambda step: sum_copy(step).start())
    sums_ref[section, replica] = send[replica]

    @pl.when(section == 0)
    def _():
        by_level(weights_done)
        by_level(across_done)
        weights_done(2)

    collect(sums_ref, 1, sum_send, sum_recv)
    loop(replicas - 1, lambda step: sum_copy(step).wait_send())


def place_kernel(lid_ref, sums_ref, out_ref):
    rows = out_ref.shape[0]
    slots = sums_ref.shape[0]
    base = pl.program_id(0) * rows
    hit = lid_ref[0:1, :] == iota((rows, slots), 0) + base
    out_ref[...] = dot(jnp.where(hit, 1.0, 0.0).astype(BF), sums_ref[...]).astype(BF)


def vmem():
    return pl.BlockSpec(memory_space=pltpu.VMEM)


def anywhere():
    return pl.BlockSpec(memory_space=pl.ANY)


def dma(*shape):
    return pltpu.SemaphoreType.DMA(shape)


def train_step(
    per_pair,
    token_ids,
    next_ids,
    embed_table,
    norm_gain,
    w_gate,
    w_up,
    w_down,
    mtp_gain,
    main_cot,
    mtp_cot,
):
    sections = lax.axis_size("section")
    replicas = lax.axis_size("dp")
    parts = lax.axis_size("mp")
    count = sections * replicas
    batches = token_ids.shape[0]
    tokens = batches * (token_ids.shape[1] // replicas)
    vocab_rows, width = embed_table.shape
    hidden = w_gate.shape[2]
    half = per_pair // 2
    slots = replicas * per_pair
    picked = min(replicas * half, max(2 * tokens, half))
    block = pltpu.VMEM((parts, tokens, width), BF)
    one = pltpu.SemaphoreType.DMA
    return pl.pallas_call(
        functools.partial(step_kernel, sections, replicas, parts, per_pair),
        out_shape=(
            jax.ShapeDtypeStruct((2, replicas, half, width), BF),
            jax.ShapeDtypeStruct((8, slots), jnp.int32),
            jax.ShapeDtypeStruct((8, 128), F32),
        ),
        in_specs=[vmem()] * 6 + [anywhere()] * 4,
        out_specs=(vmem(), vmem(), vmem()),
        scratch_shapes=[
            pltpu.VMEM((vocab_rows, width), BF),
            pltpu.VMEM((count, tokens), F32),
            pltpu.VMEM((count, tokens), F32),
            pltpu.VMEM((count, tokens), F32),
            pltpu.VMEM((slots, tokens), jnp.int32),
            pltpu.VMEM((picked, vocab_rows), BF),
            pltpu.VMEM((replicas, half, width), BF),
            pltpu.VMEM((replicas, half, width), BF),
            pltpu.VMEM((replicas, half, width), BF),
            pltpu.VMEM((2, replicas, half, width), BF),
            pltpu.VMEM((tokens, width), BF),
            pltpu.VMEM((tokens, width), BF),
            pltpu.VMEM((parts, width, 2 * hidden), BF),
            pltpu.VMEM((parts, hidden, width), BF),
            pltpu.VMEM((2, width, 2 * hidden), BF),
            pltpu.VMEM((2, hidden, width), BF),
            pltpu.VMEM((parts, tokens, 2 * hidden), BF),
            pltpu.VMEM((parts, tokens, 2 * hidden), BF),
            pltpu.VMEM((tokens, parts * hidden), BF),
            pltpu.VMEM((parts, tokens, hidden), BF),
            pltpu.VMEM((tokens, parts * hidden), BF),
            pltpu.VMEM((tokens, parts * 2 * hidden), BF),
            pltpu.VMEM((4, parts, 8, tokens), F32),
            block,
            block,
            block,
            block,
            pltpu.VMEM((2, tokens, width), BF),
            pltpu.VMEM((2, tokens, width), BF),
            pltpu.VMEM((tokens, 2 * hidden), F32),
            one,
            one,
            dma(2),
            dma(2),
            dma(replicas),
            dma(replicas),
            dma(replicas),
            dma(replicas),
            dma(2, replicas),
            dma(2, replicas),
            dma(3),
            dma(3, parts),
            dma(3, parts),
            dma(3, parts),
            dma(3, 2),
            dma(3, 2),
            dma(parts),
        ]
        + [dma(parts)] * 8
        + [dma(4, parts)] * 2
        + [one] * 2
        + [dma(parts)] * 6
        + [dma(2)],
        compiler_params=pltpu.CompilerParams(
            collective_id=0 if per_pair == FEW_SLOTS else 1,
            has_side_effects=True,
            vmem_limit_bytes=60 << 20,
        ),
        name=f"train_step_{per_pair}",
    )(
        token_ids,
        next_ids,
        main_cot.reshape(tokens, width),
        mtp_cot.reshape(tokens, width),
        norm_gain,
        mtp_gain,
        embed_table,
        w_gate[0],
        w_up[0],
        w_down[0],
    )


def place(lid_row, sums, vocab_rows):
    width = sums.shape[-1]
    slots = lid_row.shape[1]
    block = vocab_rows // 8
    return pl.pallas_call(
        place_kernel,
        grid=(vocab_rows // block,),
        out_shape=jax.ShapeDtypeStruct((vocab_rows, width), BF),
        in_specs=[
            pl.BlockSpec((8, slots), lambda i: (0, 0)),
            pl.BlockSpec((slots, width), lambda i: (0, 0)),
        ],
        out_specs=pl.BlockSpec((block, width), lambda i: (i, 0)),
        compiler_params=pltpu.CompilerParams(vmem_limit_bytes=56 << 20),
        name="place_rows",
    )(lid_row, sums.reshape(slots, width))


def body(*arguments):
    vocab_rows = arguments[2].shape[0]
    positions = 2 * arguments[0].shape[0] * (arguments[0].shape[1] // lax.axis_size("dp"))
    sums, lid_row, most = train_step(FEW_SLOTS, *arguments)

    def few(sums, lid_row, *given):
        return place(lid_row, sums, vocab_rows)

    def many(sums, lid_row, *given):
        sums, lid_row, most = train_step(positions, *given)
        return place(lid_row, sums, vocab_rows)

    return lax.cond(most[0, 0] <= FEW_SLOTS, few, many, sums, lid_row, *arguments)


def solution(mesh):
    return jax.shard_map(
        body,
        mesh=mesh,
        in_specs=(
            P(),
            P(),
            P(("section", "dp"), "mp"),
            P("section", None),
            P("section", None, "mp"),
            P("section", None, "mp"),
            P("section", "mp", None),
            P(),
            P(None, "dp", "mp"),
            P(None, "dp", "mp"),
        ),
        out_specs=P(("section", "dp"), "mp"),
        check_vma=False,
    )
```
